256 devices in a mesh: row: 8 (over z_lo, y), col: 32 (over z_hi, x, core).
Axes of the slice: x: 4, y: 4, z: 8 (z_hi: 4, z_lo: 2; z = z_hi * 2 + z_lo), core: 2. Of those that a mesh axis runs over, the one named last changes fastest.
Arguments:
- eigvecs: float32 [32768, 4096], P(('row', 'col')), may hold values from -6 to 6
- householder: float32 [5, 32768, 256], P(None, 'row', 'col'), may hold values from -0.375 to 0.375
- tfactor: float32 [5, 256, 256], replicated, may hold values from -0.02 to 0.03, as said below
Outputs:
- transformed: float32 [32768, 4096], P('row', 'col')
The draws below stay inside these ranges and needn't reach their ends.
Inputs may be any that keep to these rules, and one draw needn't show every extreme that they name: tfactor[b] is upper triangular with a positive diagonal.
All inputs are finite; a program needn't handle non-finite values.
Results may differ from the reference program's by a relative error of at most 0.0001.
Values sent between devices are 32-bit elements; how exact they have to be, the bound alone decides.
No kernel may reach another device: no remote copies, remote signals or barrier semaphores. Data moves between devices by JAX's collectives and lax.ppermute only.
A program may use at most 128 MiB of HBM per device.

```python
import jax
import jax.numpy as jnp
from jax import lax

N = 32768
NB = 256
BLOCKS = 5
K = 4096


def draw_tfactor(key, part):
    first = jax.random.fold_in(key, 11)
    second = jax.random.fold_in(key, 23)
    diagonal = jax.random.uniform(first, (BLOCKS, NB), jnp.float32, 0.008, 0.024)
    upper = jnp.clip(jax.random.normal(second, (BLOCKS, NB, NB), jnp.float32) * 0.004, -0.02, 0.02)
    return jnp.triu(upper, 1) + diagonal[:, :, None] * jnp.eye(NB, dtype=jnp.float32)


def block_scale(own_key, shape, split, smallest, high):
    loudness, own = 1.0, jax.random.fold_in(own_key, 6)
    for dim, parts in split:
        draws = jnp.exp(jax.random.uniform(jax.random.fold_in(own, dim), (parts,), jnp.float32, smallest / len(split), high / len(split)))
        loudness = loudness * jnp.repeat(draws, shape[dim] // parts).reshape([-1 if axis == dim else 1 for axis in range(len(shape))])
    return loudness


def gaussian(stream_key, extent, scale, limit, pieces=(), kind=jnp.bfloat16):
    drawn = scale * jax.random.normal(stream_key, extent, jnp.float32)
    if pieces:
        drawn = drawn * block_scale(stream_key, extent, pieces, -0.22, 0.18)
    return jnp.clip(drawn, -limit, limit).astype(kind)


def setup_inputs(seed: int = 0) -> dict:
    key_list = jax.random.split(jax.random.key(seed), 4)
    return {
        "eigvecs": gaussian(key_list[0], (N, K), 1.0, 6.0, ((0, 256),), jnp.float32),
        "householder": gaussian(key_list[1], (BLOCKS, N, NB), NB ** -0.5, 0.375, ((1, 8), (2, 32)), jnp.float32),
        "tfactor": draw_tfactor(jax.random.fold_in(key_list[3], 71), 0),
    }


def reference(eigvecs, householder, tfactor):
    current = eigvecs
    for number in range(BLOCKS - 1, -1, -1):
        vectors = householder[number]
        projected = lax.dot_general(vectors, current, (((0,), (0,)), ((), ())), precision=lax.Precision.HIGHEST, preferred_element_type=jnp.float32)
        applied = jnp.dot(tfactor[number], projected, precision=lax.Precision.HIGHEST, preferred_element_type=jnp.float32)
        current = current - jnp.dot(vectors, applied, precision=lax.Precision.HIGHEST, preferred_element_type=jnp.float32)
    return current
```

```python
import functools

import jax
import jax.numpy as jnp
from jax import lax
from jax.experimental import pallas as pl
from jax.experimental.pallas import tpu as pltpu
from jax.sharding import Mesh
from jax.sharding import PartitionSpec as P

AXES = ("zl", "y", "zh", "x", "core")
SIZES = (2, 4, 4, 4, 2)
ROW, COL = ("zl", "y"), ("zh", "x", "core")
RING = 4
ROWS = 4096
NB = 256
K = 128
STEP = 512
HIGHEST = lax.Precision.HIGHEST
GROUPS = ((4, 3), (2, 1), (0,))


def shift(a, axis, by):
    n = SIZES[AXES.index(axis)]
    return lax.ppermute(a, axis, [(i, (i + by) % n) for i in range(n)])


def both_ways(a, axis):
    pairs = []
    for i in range(RING):
        pairs.append((i * 2, ((i + 1) % RING) * 2))
        pairs.append((i * 2 + 1, ((i - 1) % RING) * 2 + 1))
    return lax.ppermute(a, (axis, "core"), pairs)


def swap(a):
    return shift(a, "core", 1)


def gather_z(v):
    n = v.shape[0]
    other = swap(v)
    near = both_ways(jnp.concatenate([v, other], 0), "zh")
    far = both_ways(near[:n], "zh")
    mine = (v, near[:n], near[n:], far)
    got = swap(jnp.concatenate([near, far], 0))
    theirs = (other, got[:n], got[n : 2 * n], got[2 * n :])
    return mine, theirs


def gather_x(full):
    half = full.shape[0] // 2
    near = both_ways(full, "x")
    far = both_ways(near[:half], "x")
    return (full, near, far, swap(near), swap(far))


def column_order():
    z, x, c = (lax.axis_index(a) for a in COL)
    s = 1 - 2 * c
    d, s2 = 1 - c, 2 * c - 1

    def half(core, sign):
        return [(z, core), (z - sign, core), (z - sign, 1 - core), (z + 2, core)]

    mine, theirs = half(c, s), half(d, s2)
    order = [(x, o) for o in mine + theirs]
    order += [(x - s, o) for o in mine + theirs]
    order += [(x + 2, o) for o in mine]
    order += [(x + s, o) for o in theirs + mine]
    order += [(x + 2, o) for o in theirs]
    unit = jnp.stack([((zz % 4) * 4 + xx % 4) * 2 + cc for xx, (zz, cc) in order])
    return (unit[:, None] * 8 + jnp.arange(8)[None, :]).reshape(NB)


def place_kernel(where, s0, s1, s2, s3, out):
    for e, s in enumerate((s0, s1, s2, s3)):
        for d in range(RING):
            at = pl.multiple_of(where[e * RING + d] * 256, 256)
            out[:, pl.ds(at, 256)] = s[d]


def exchange(eigvecs):
    z, x, c = (lax.axis_index(a) for a in COL)
    e = eigvecs.T.reshape(16, 2, K, 128)
    keep = lax.dynamic_index_in_dim(e, c, 1, keepdims=False)
    give = lax.dynamic_index_in_dim(e, 1 - c, 1, keepdims=False)
    got = swap(give)
    first = jnp.where(c == 0, keep, got)
    second = jnp.where(c == 0, got, keep)
    h = jnp.concatenate([first, second], -1).reshape(4, 4, K, 256)
    parts = []
    for d in range(RING):
        piece = lax.dynamic_index_in_dim(h, (x + d) % 4, 1, keepdims=False)
        parts.append(shift(piece, "x", d) if d else piece)
    f = jnp.stack(parts, 1)
    out = []
    for d in range(RING):
        piece = lax.dynamic_index_in_dim(f, (z + d) % 4, 0, keepdims=False)
        out.append(shift(piece, "zh", d) if d else piece)
    where = jnp.stack([((z - i) % 4) * 4 + (x - j) % 4 for i in range(4) for j in range(4)])
    return pl.pallas_call(
        place_kernel,
        grid_spec=pltpu.PrefetchScalarGridSpec(
            num_scalar_prefetch=1,
            grid=(1,),
            in_specs=[pl.BlockSpec((4, K, 256), lambda i, w: (0, 0, 0))] * 4,
            out_specs=pl.BlockSpec((K, ROWS), lambda i, w: (0, 0)),
        ),
        out_shape=jax.ShapeDtypeStruct((K, ROWS), jnp.float32),
        compiler_params=pltpu.CompilerParams(vmem_limit_bytes=24 << 20),
        cost_estimate=pl.CostEstimate(flops=0, bytes_accessed=4 << 20, transcendentals=0),
        name="place",
    )(where.astype(jnp.int32), *out)


def spread(w):
    w = w + shift(w, "zl", 1)
    return w + shift(w, "y", 1) + shift(w, "y", 2) + shift(w, "y", 3)


def split(a):
    hi = a.astype(jnp.bfloat16)
    return hi, (a - hi.astype(jnp.float32)).astype(jnp.bfloat16)


def dot(a, b, dims):
    return lax.dot_general(a, b, (dims, ((), ())), preferred_element_type=jnp.float32)


def product(a, b, dims):
    (ah, al), (bh, bl) = a, b
    return dot(ah, bh, dims) + (dot(ah, bl, dims) + dot(al, bh, dims))


NT = ((1,), (1,))
NN = ((1,), (0,))


def stacked(refs):
    return jnp.concatenate([r[...] for r in refs], 0)


def work_kernel(n_old, n_new, last, *refs):
    cur_ref, refs = refs[0], refs[1:]
    cur = cur_ref[...]
    if n_old:
        applied, refs = split(refs[0][...]), refs[1:]
        old, refs = split(stacked(refs[: 5 * n_old])), refs[5 * n_old :]
        cur = cur - product(applied, old, NN)
    if last:
        refs[0][...] = cur.T
        return
    new, refs = split(stacked(refs[: 5 * n_new])), refs[5 * n_new :]
    if n_old:
        refs[0][...] = cur
        refs = refs[1:]
    w_ref = refs[0]
    part = product(new, split(cur), NT)

    @pl.when(pl.program_id(0) == 0)
    def _():
        w_ref[...] = part

    @pl.when(pl.program_id(0) != 0)
    def _():
        w_ref[...] += part


def piece_specs(pieces):
    return [pl.BlockSpec((p.shape[0], STEP), lambda i: (0, i)) for p in pieces]


def work(cur, applied, old, new):
    n_old, n_new = len(old), len(new)
    last = not new
    old, new = sum(old, ()), sum(new, ())
    args, specs = [cur], [pl.BlockSpec((K, STEP), lambda i: (0, i))]
    if n_old:
        args += [applied, *old]
        specs += [pl.BlockSpec((K, NB * n_old), lambda i: (0, 0))] + piece_specs(old)
    args += new
    specs += piece_specs(new)
    shapes, outs = [], []
    if last:
        shapes.append(jax.ShapeDtypeStruct((ROWS, K), jnp.float32))
        outs.append(pl.BlockSpec((STEP, K), lambda i: (i, 0)))
    elif n_old:
        shapes.append(jax.ShapeDtypeStruct((K, ROWS), jnp.float32))
        outs.append(pl.BlockSpec((K, STEP), lambda i: (0, i)))
    if not last:
        shapes.append(jax.ShapeDtypeStruct((NB * n_new, K), jnp.float32))
        outs.append(pl.BlockSpec((NB * n_new, K), lambda i: (0, 0)))
    n = n_old + n_new
    return pl.pallas_call(
        functools.partial(work_kernel, n_old, n_new, last),
        grid=(ROWS // STEP,),
        in_specs=specs,
        out_specs=outs,
        out_shape=shapes,
        compiler_params=pltpu.CompilerParams(vmem_limit_bytes=40 << 20),
        cost_estimate=pl.CostEstimate(
            flops=6 * n * NB * K * ROWS, bytes_accessed=4 * ROWS * (n * NB + 2 * K), transcendentals=0
        ),
        name="work",
    )(*args)


def overlap_kernel(*refs):
    g_ref = refs[-1]
    low, high = split(stacked(refs[:5])), split(stacked(refs[5:10]))
    part = product(low, high, NT)

    @pl.when(pl.program_id(0) == 0)
    def _():
        g_ref[...] = part

    @pl.when(pl.program_id(0) != 0)
    def _():
        g_ref[...] += part


def overlap(low, high):
    return pl.pallas_call(
        overlap_kernel,
        grid=(ROWS // STEP,),
        in_specs=piece_specs(low) + piece_specs(high),
        out_specs=pl.BlockSpec((NB, NB), lambda i: (0, 0)),
        out_shape=jax.ShapeDtypeStruct((NB, NB), jnp.float32),
        compiler_params=pltpu.CompilerParams(vmem_limit_bytes=40 << 20),
        cost_estimate=pl.CostEstimate(
            flops=6 * NB * NB * ROWS, bytes_accessed=8 * ROWS * NB, transcendentals=0
        ),
        name="overlap",
    )(*low, *high)


def exact(a, b):
    return lax.dot_general(a, b, (NN, ((), ())), precision=HIGHEST, preferred_element_type=jnp.float32)


def solve_kernel(n, *refs):
    t_ref, w_ref, out = refs[0], refs[1], refs[-1]
    first = exact(t_ref[0], w_ref[:NB])
    out[:, :NB] = first.T
    if n == 2:
        g_ref = refs[2]
        out[:, NB:] = exact(t_ref[1], w_ref[NB:] - exact(g_ref[...], first)).T


def solve(t, w, *g):
    n = t.shape[0]
    return pl.pallas_call(
        functools.partial(solve_kernel, n),
        out_shape=jax.ShapeDtypeStruct((K, NB * n), jnp.float32),
        cost_estimate=pl.CostEstimate(flops=12 * n * NB * NB * K, bytes_accessed=1 << 20, transcendentals=0),
        compiler_params=pltpu.CompilerParams(vmem_limit_bytes=24 << 20),
        name="solve",
    )(t, w, *g)


def on_device(eigvecs, householder, tfactor):
    v = jnp.swapaxes(householder, 1, 2)
    pick = (column_order()[:, None] == jnp.arange(NB)[None, :]).astype(jnp.float32)
    t = jnp.einsum("ij,bjk,lk->bil", pick, tfactor, pick, precision=HIGHEST)

    pieces = {}
    for b in (4, 3, 2, 1, 0):
        mine, theirs = gather_z(v[b])
        pieces[b] = gather_x(jnp.concatenate(mine + theirs, 0))
    cur = exchange(eigvecs)

    applied, old = None, ()
    for group in GROUPS:
        new = tuple(pieces[b] for b in group)
        res = work(cur, applied, old, new)
        if old:
            cur, w = res
        else:
            (w,) = res
        g = [spread(overlap(pieces[group[1]], pieces[group[0]]))] if len(group) == 2 else []
        tg = jnp.stack([t[b] for b in group])
        applied = solve(tg, spread(w), *g)
        old = new
    return work(cur, applied, old, ())[0]


def solution(mesh):
    fine = Mesh(mesh.devices.reshape(SIZES), AXES)
    placed = (P(ROW + COL, None), P(None, ROW, COL), P())
    return jax.shard_map(on_device, mesh=fine, in_specs=placed, out_specs=P(ROW, COL), check_vma=False)
```

```python
import functools

import jax
import jax.numpy as jnp
from jax import lax
from jax.experimental import pallas as pl
from jax.experimental.pallas import tpu as pltpu
from jax.sharding import Mesh
from jax.sharding import PartitionSpec as P

AXES = ("zl", "y", "zh", "x", "core")
SIZES = (2, 4, 4, 4, 2)
ROW, COL = ("zl", "y"), ("zh", "x", "core")
RING = 4
ROWS = 4096
NB = 256
K = 128
STEP = 512
HIGHEST = lax.Precision.HIGHEST


def tie(a, *events):
    return lax.optimization_barrier((a, *events))[0] if events else a


def shift(a, axis, by):
    n = SIZES[AXES.index(axis)]
    return lax.ppermute(a, axis, [(i, (i + by) % n) for i in range(n)])


def both_ways(a, axis):
    pairs = []
    for i in range(RING):
        pairs.append((i * 2, ((i + 1) % RING) * 2))
        pairs.append((i * 2 + 1, ((i - 1) % RING) * 2 + 1))
    return lax.ppermute(a, (axis, "core"), pairs)


def swap(a):
    return shift(a, "core", 1)


def gather_x(full, before=(), between=()):
    half = full.shape[0] // 2
    near = both_ways(tie(full, *before), "x")
    far = both_ways(tie(near[:half], *between), "x")
    return (full, near, far, swap(near), swap(far))


def chunks(n, i):
    return (i, n + i, 2 * n + i, 3 * n + i, 4 * n + i, 5 * n + i, 6 * n + i, 7 * n + i)


def column_order():
    x, c = lax.axis_index("x"), lax.axis_index("core")
    s = 1 - 2 * c
    order = [(x, c), (x, 1 - c), (x - s, c), (x - s, 1 - c), (x + 2, c)]
    order += [(x + s, 1 - c), (x + s, c), (x + 2, 1 - c)]
    unit = jnp.stack([(z * 4 + xx % 4) * 2 + cc for xx, cc in order for z in range(4)])
    return (unit[:, None] * 8 + jnp.arange(8)[None, :]).reshape(NB)


def exchange(eigvecs):
    return lax.all_to_all(eigvecs.T.reshape(32, K, 128), COL, split_axis=0, concat_axis=0, tiled=True)


def row_sum(a):
    n, width = a.shape
    a = lax.all_to_all(a.reshape(8, n // 8, width), ROW, split_axis=0, concat_axis=0, tiled=True)
    a = jnp.broadcast_to(jnp.sum(a, 0), a.shape)
    return lax.all_to_all(a, ROW, split_axis=0, concat_axis=0, tiled=True).reshape(n, width)


def split(a):
    hi = a.astype(jnp.bfloat16)
    return hi, (a - hi.astype(jnp.float32)).astype(jnp.bfloat16)


def dot(a, b, dims):
    return lax.dot_general(a, b, (dims, ((), ())), preferred_element_type=jnp.float32)


def product(a, b, dims):
    (ah, al), (bh, bl) = a, b
    return dot(ah, bh, dims) + (dot(ah, bl, dims) + dot(al, bh, dims))


NT = ((1,), (1,))
NN = ((1,), (0,))


def stacked(refs):
    return jnp.concatenate([r[...] for r in refs], 0)


def work_kernel(has_old, has_new, *refs):
    cur_ref, refs = refs[0], refs[1:]
    cur = cur_ref[...] if len(cur_ref.shape) == 2 else jnp.concatenate([cur_ref[i] for i in range(STEP // 128)], 1)
    if has_old:
        applied, old, refs = split(refs[0][...]), split(stacked(refs[1:6])), refs[6:]
        cur = cur - product(applied, old, NN)
    if not has_new:
        refs[0][...] = cur.T
        return
    new, refs = split(stacked(refs[:5])), refs[5:]
    if has_old:
        refs[0][...] = cur
        refs = refs[1:]
    w_ref = refs[0]
    part = product(new, split(cur), NT)

    @pl.when(pl.program_id(0) == 0)
    def _():
        w_ref[...] = part

    @pl.when(pl.program_id(0) != 0)
    def _():
        w_ref[...] += part


def piece_specs(pieces):
    return [pl.BlockSpec((p.shape[0], STEP), lambda i: (0, i)) for p in pieces]


def rows_of(pieces):
    return sum(p.shape[0] for p in pieces)


def work(cur, applied, old, new):
    args, specs = [cur], [pl.BlockSpec((K, STEP), lambda i: (0, i))]
    if cur.ndim == 3:
        specs = [pl.BlockSpec((STEP // 128, K, 128), lambda i: (i, 0, 0))]
    if old:
        args += [applied, *old]
        specs += [pl.BlockSpec(applied.shape, lambda i: (0, 0))] + piece_specs(old)
    args += new
    specs += piece_specs(new)
    shapes, outs = [], []
    if not new:
        shapes.append(jax.ShapeDtypeStruct((ROWS, K), jnp.float32))
        outs.append(pl.BlockSpec((STEP, K), lambda i: (i, 0)))
    elif old:
        shapes.append(jax.ShapeDtypeStruct((K, ROWS), jnp.float32))
        outs.append(pl.BlockSpec((K, STEP), lambda i: (0, i)))
    if new:
        shapes.append(jax.ShapeDtypeStruct((rows_of(new), K), jnp.float32))
        outs.append(pl.BlockSpec((rows_of(new), K), lambda i: (0, 0)))
    n = rows_of(old) + rows_of(new)
    return pl.pallas_call(
        functools.partial(work_kernel, bool(old), bool(new)),
        grid=(ROWS // STEP,),
        in_specs=specs,
        out_specs=outs,
        out_shape=shapes,
        compiler_params=pltpu.CompilerParams(vmem_limit_bytes=40 << 20),
        cost_estimate=pl.CostEstimate(
            flops=6 * n * K * ROWS, bytes_accessed=4 * ROWS * (n + 2 * K), transcendentals=0
        ),
        name="work",
    )(*args)


def block_of(a, i, n):
    return jnp.concatenate([a[32 * k : 32 * k + 32] for k in chunks(n, i)], 0)


def overlap_kernel(*refs):
    g_ref = refs[-1]
    both = stacked(refs[:5])
    part = product(split(block_of(both, 1, 2)), split(block_of(both, 0, 2)), NT)

    @pl.when(pl.program_id(0) == 0)
    def _():
        g_ref[...] = part

    @pl.when(pl.program_id(0) != 0)
    def _():
        g_ref[...] += part


def overlap(pieces):
    return pl.pallas_call(
        overlap_kernel,
        grid=(ROWS // STEP,),
        in_specs=piece_specs(pieces),
        out_specs=pl.BlockSpec((NB, NB), lambda i: (0, 0)),
        out_shape=jax.ShapeDtypeStruct((NB, NB), jnp.float32),
        compiler_params=pltpu.CompilerParams(vmem_limit_bytes=40 << 20),
        cost_estimate=pl.CostEstimate(
            flops=6 * NB * NB * ROWS, bytes_accessed=8 * ROWS * NB, transcendentals=0
        ),
        name="overlap",
    )(*pieces)


def exact(a, b):
    return lax.dot_general(a, b, (NN, ((), ())), precision=HIGHEST, preferred_element_type=jnp.float32)


def solve_kernel(n, *refs):
    t_ref, w_ref, out = refs[0], refs[1], refs[-1]
    w = w_ref[...]
    done = [exact(t_ref[0], block_of(w, 0, n))]
    if n == 2:
        done.append(exact(t_ref[1], block_of(w, 1, n) - exact(refs[2][...], done[0])))
    laid = sorted((k, i, j) for i in range(n) for j, k in enumerate(chunks(n, i)))
    out[...] = jnp.concatenate([done[i][32 * j : 32 * j + 32] for _, i, j in laid], 0).T


def solve(t, w, *g):
    n = t.shape[0]
    return pl.pallas_call(
        functools.partial(solve_kernel, n),
        out_shape=jax.ShapeDtypeStruct((K, NB * n), jnp.float32),
        cost_estimate=pl.CostEstimate(flops=12 * n * NB * NB * K, bytes_accessed=1 << 20, transcendentals=0),
        compiler_params=pltpu.CompilerParams(vmem_limit_bytes=24 << 20),
        name="solve",
    )(t, w, *g)


def on_device(eigvecs, householder, tfactor):
    v = jnp.swapaxes(householder, 1, 2)

    def gather_z(blocks):
        mine = jnp.stack([v[b] for b in blocks])
        return lax.all_gather(mine, "zh", axis=1).reshape(32 * len(blocks), ROWS)

    def full(half):
        return jnp.concatenate([half, swap(half)], 0)

    first, rest = gather_z((4, 3)), gather_z((2, 1, 0))
    pick = (column_order()[:, None] == jnp.arange(NB)[None, :]).astype(jnp.float32)
    t = jnp.einsum("ij,bjk,lk->bil", pick, tfactor, pick, precision=HIGHEST)
    ts = [jnp.stack([t[b] for b in group]) for group in ((4, 3), (2, 1), (0,))]

    cur = exchange(eigvecs)
    pieces = [gather_x(full(first), (cur,))]
    pieces.append(gather_x(full(rest[:64]), (pieces[0][1],), (pieces[0][2],)))
    pieces.append(gather_x(full(rest[64:]), (pieces[1][1],), (pieces[1][2],)))

    applied, old, g = None, (), [row_sum(overlap(pieces[0]))]
    for group, new in enumerate(pieces):
        res = work(cur, applied, old, new)
        if old:
            cur, w = res
        else:
            (w,) = res
        w = row_sum(w)
        after = [overlap(pieces[1])] if group == 0 else []
        applied = solve(ts[group], tie(w, *after), *g)
        old, g = new, [row_sum(a) for a in after]
    return work(cur, applied, old, ())[0]


def solution(mesh):
    fine = Mesh(mesh.devices.reshape(SIZES), AXES)
    placed = (P(ROW + COL, None), P(None, ROW, COL), P())
    return jax.shard_map(on_device, mesh=fine, in_specs=placed, out_specs=P(ROW, COL), check_vma=False)
```

```python
import functools

import jax
import jax.numpy as jnp
from jax import lax
from jax.experimental import pallas as pl
from jax.experimental.pallas import tpu as pltpu
from jax.sharding import Mesh
from jax.sharding import PartitionSpec as P

AXES = ("zl", "y", "zh", "x", "core")
SIZES = (2, 4, 4, 4, 2)
ROW, COL = ("zl", "y"), ("zh", "x", "core")
RING = 4
ROWS = 4096
NB = 256
K = 128
STEP = 1024
HIGHEST = lax.Precision.HIGHEST


def tie(a, *events):
    return lax.optimization_barrier((a, *events))[0] if events else a


def shift(a, axis, by):
    n = SIZES[AXES.index(axis)]
    return lax.ppermute(a, axis, [(i, (i + by) % n) for i in range(n)])


def both_ways(a, axis):
    pairs = []
    for i in range(RING):
        pairs.append((i * 2, ((i + 1) % RING) * 2))
        pairs.append((i * 2 + 1, ((i - 1) % RING) * 2 + 1))
    return lax.ppermute(a, (axis, "core"), pairs)


def swap(a):
    return shift(a, "core", 1)


def gather_z(v, other, *events):
    n = v.shape[0]
    near = both_ways(tie(jnp.concatenate([v, other], 0), *events), "zh")
    far = both_ways(near[:n], "zh")
    got = swap(jnp.concatenate([near, far], 0))
    mine = by_block((v, near[:n], near[n:], far))
    theirs = by_block((other, got[:n], got[n : 2 * n], got[2 * n :]))
    return jnp.concatenate([mine, theirs], 0), near


def by_block(parts):
    n = parts[0].shape[0] // 8
    return jnp.stack([p.reshape(n, 8, ROWS) for p in parts], 1).reshape(32 * n, ROWS)


def gather_x(full, before=(), between=()):
    half = full.shape[0] // 2
    near = both_ways(tie(full, *before), "x")
    far = both_ways(tie(near[:half], *between), "x")
    return (full, near, far, swap(near), swap(far))


def chunks(n, i):
    return (i, n + i, 2 * n + i, 3 * n + i, 4 * n + i, 5 * n + i, 6 * n + i, 7 * n + i)


def column_order(ring):
    z, x, c = (lax.axis_index(a) for a in COL)
    s = 1 - 2 * c

    def half(core, sign):
        if ring:
            return [(z, core), (z - sign, core), (z - sign, 1 - core), (z + 2, core)]
        return [(i, core) for i in range(4)]

    mine, theirs = half(c, s), half(1 - c, -s)
    order = [(x, mine), (x, theirs), (x - s, mine), (x - s, theirs), (x + 2, mine)]
    order += [(x + s, theirs), (x + s, mine), (x + 2, theirs)]
    unit = jnp.stack([((zz % 4) * 4 + xx % 4) * 2 + cc for xx, units in order for zz, cc in units])
    return (unit[:, None] * 8 + jnp.arange(8)[None, :]).reshape(NB)


def exchange(eigvecs):
    return lax.all_to_all(eigvecs.T.reshape(32, K, 128), COL, split_axis=0, concat_axis=0, tiled=True)


def row_sum(a):
    n, width = a.shape
    a = lax.all_to_all(a.reshape(8, n // 8, width), ROW, split_axis=0, concat_axis=0, tiled=True)
    a = jnp.broadcast_to(jnp.sum(a, 0), a.shape)
    return lax.all_to_all(a, ROW, split_axis=0, concat_axis=0, tiled=True).reshape(n, width)


def row_sum_small(w):
    w = w + shift(w, "zl", 1)
    return w + shift(w, "y", 1) + shift(w, "y", 2) + shift(w, "y", 3)


def split(a):
    hi = a.astype(jnp.bfloat16)
    return hi, (a - hi.astype(jnp.float32)).astype(jnp.bfloat16)


def dot(a, b, dims):
    return lax.dot_general(a, b, (dims, ((), ())), preferred_element_type=jnp.float32)


NT = ((1,), (1,))
NN = ((1,), (0,))


def project(v, cur):
    (vh, vl), (ch, cl) = v, cur
    n = ch.shape[0]
    both = dot(vh, jnp.concatenate([ch, cl], 0), NT)
    return both[:, :n] + both[:, n:] + dot(vl, ch, NT)


def spread_out(applied, v):
    (ah, al), (vh, vl) = applied, v
    both = dot(jnp.concatenate([ah, al], 0), vh, NN)
    return both[:K] + both[K:] + dot(ah, vl, NN)


def stacked(refs):
    return jnp.concatenate([r[...] for r in refs], 0)


def block_of(a, i, n):
    return jnp.concatenate([a[32 * k : 32 * k + 32] for k in chunks(n, i)], 0)


def work_kernel(has_old, has_new, *refs):
    cur_ref, refs = refs[0], refs[1:]
    cur = cur_ref[...] if len(cur_ref.shape) == 2 else jnp.concatenate([cur_ref[i] for i in range(STEP // 128)], 1)
    if has_old:
        applied, old, refs = split(refs[0][...]), split(stacked(refs[1:6])), refs[6:]
        cur = cur - spread_out(applied, old)
    if not has_new:
        refs[0][...] = cur.T
        return
    new, refs = stacked(refs[:5]), refs[5:]
    if has_old:
        refs[0][...] = cur
        refs = refs[1:]
    w_ref = refs[0]
    if new.shape[0] == NB:
        part = project(split(new), split(cur))
    else:
        high, low = split(new)
        first, second = ((block_of(high, i, 2), block_of(low, i, 2)) for i in range(2))
        now = split(cur)
        g = project(second, first)
        part = jnp.concatenate([project(first, now), project(second, now), g[:, :K], g[:, K:]], 0)

    @pl.when(pl.program_id(0) == 0)
    def _():
        w_ref[...] = part

    @pl.when(pl.program_id(0) != 0)
    def _():
        w_ref[...] += part


def piece_specs(pieces):
    return [pl.BlockSpec((p.shape[0], STEP), lambda i: (0, i)) for p in pieces]


def rows_of(pieces):
    return sum(p.shape[0] for p in pieces)


def work(cur, applied, old, new):
    args, specs = [cur], [pl.BlockSpec((K, STEP), lambda i: (0, i))]
    if cur.ndim == 3:
        specs = [pl.BlockSpec((STEP // 128, K, 128), lambda i: (i, 0, 0))]
    if old:
        args += [applied, *old]
        specs += [pl.BlockSpec(applied.shape, lambda i: (0, 0))] + piece_specs(old)
    args += new
    specs += piece_specs(new)
    shapes, outs = [], []
    if not new:
        shapes.append(jax.ShapeDtypeStruct((ROWS, K), jnp.float32))
        outs.append(pl.BlockSpec((STEP, K), lambda i: (i, 0)))
    elif old:
        shapes.append(jax.ShapeDtypeStruct((K, ROWS), jnp.float32))
        outs.append(pl.BlockSpec((K, STEP), lambda i: (0, i)))
    if new:
        n = 1024 if rows_of(new) > NB else NB
        shapes.append(jax.ShapeDtypeStruct((n, K), jnp.float32))
        outs.append(pl.BlockSpec((n, K), lambda i: (0, 0)))
    n = rows_of(old) + rows_of(new)
    return pl.pallas_call(
        functools.partial(work_kernel, bool(old), bool(new)),
        grid=(ROWS // STEP,),
        in_specs=specs,
        out_specs=outs,
        out_shape=shapes,
        compiler_params=pltpu.CompilerParams(vmem_limit_bytes=50 << 20),
        cost_estimate=pl.CostEstimate(
            flops=6 * n * K * ROWS, bytes_accessed=4 * ROWS * (n + 2 * K), transcendentals=0
        ),
        name="work",
    )(*args)


def exact(a, b):
    return lax.dot_general(a, b, (NN, ((), ())), precision=HIGHEST, preferred_element_type=jnp.float32)


def solve_kernel(n, t_ref, w_ref, out):
    done = [exact(t_ref[0], w_ref[:NB])]
    if n == 2:
        g = exact(w_ref[2 * NB : 3 * NB], done[0][:K]) + exact(w_ref[3 * NB :], done[0][K:])
        done.append(exact(t_ref[1], w_ref[NB : 2 * NB] - g))
    laid = sorted((k, i, j) for i in range(n) for j, k in enumerate(chunks(n, i)))
    out[...] = jnp.concatenate([done[i][32 * j : 32 * j + 32] for _, i, j in laid], 0).T


def solve(t, w):
    n = t.shape[0]
    return pl.pallas_call(
        functools.partial(solve_kernel, n),
        out_shape=jax.ShapeDtypeStruct((K, NB * n), jnp.float32),
        cost_estimate=pl.CostEstimate(flops=12 * n * NB * NB * K, bytes_accessed=1 << 20, transcendentals=0),
        compiler_params=pltpu.CompilerParams(vmem_limit_bytes=24 << 20),
        name="solve",
    )(t, w)


def on_device(eigvecs, householder, tfactor):
    v = jnp.swapaxes(householder, 1, 2)

    v43 = jnp.concatenate([v[4], v[3]], 0)
    rest = jnp.stack([v[2], v[1], v[0]])
    full43, _ = gather_z(v43, swap(v43), rest)
    rest = lax.all_gather(rest, "zh", axis=1).reshape(96, ROWS)

    def full(half):
        return jnp.concatenate([half, swap(half)], 0)

    cur = exchange(eigvecs)
    pieces = [gather_x(full43)]
    pieces.append(gather_x(full(rest[:64]), (pieces[0][1], cur), (pieces[0][2],)))
    pieces.append(gather_x(full(rest[64:]), (pieces[1][1],), (pieces[1][2],)))

    def ordered(ring, *blocks):
        pick = (column_order(ring)[:, None] == jnp.arange(NB)[None, :]).astype(jnp.float32)
        part = jnp.stack([tfactor[b] for b in blocks])
        return jnp.einsum("ij,bjk,lk->bil", pick, part, pick, precision=HIGHEST)

    ts = [ordered(True, 4, 3), ordered(False, 2, 1), ordered(False, 0)]

    applied, old = None, ()
    for t, new in zip(ts, pieces):
        res = work(cur, applied, old, new)
        if old:
            cur, w = res
        else:
            (w,) = res
        applied = solve(t, row_sum(w) if len(t) == 2 else row_sum_small(w))
        old = new
    return work(cur, applied, old, ())[0]


def solution(mesh):
    fine = Mesh(mesh.devices.reshape(SIZES), AXES)
    placed = (P(ROW + COL, None), P(None, ROW, COL), P())
    return jax.shard_map(on_device, mesh=fine, in_specs=placed, out_specs=P(ROW, COL), check_vma=False)
```

```python
import functools

import jax
import jax.numpy as jnp
from jax import lax
from jax.experimental import pallas as pl
from jax.experimental.pallas import tpu as pltpu
from jax.sharding import Mesh
from jax.sharding import PartitionSpec as P

AXES = ("zl", "y", "zh", "x", "core")
SIZES = (2, 4, 4, 4, 2)
ROW, COL = ("zl", "y"), ("zh", "x", "core")
RING = 4
ROWS = 4096
NB = 256
K = 128
STEP = 1024
HIGHEST = lax.Precision.HIGHEST


def tie(a, *events):
    return lax.optimization_barrier((a, *events))[0] if events else a


def shift(a, axis, by):
    n = SIZES[AXES.index(axis)]
    return lax.ppermute(a, axis, [(i, (i + by) % n) for i in range(n)])


def both_ways(a, axis):
    pairs = []
    for i in range(RING):
        pairs.append((i * 2, ((i + 1) % RING) * 2))
        pairs.append((i * 2 + 1, ((i - 1) % RING) * 2 + 1))
    return lax.ppermute(a, (axis, "core"), pairs)


def swap(a):
    return shift(a, "core", 1)


def gather_z(v, other, before=(), between=(), after=()):
    n = v.shape[0]
    near = both_ways(tie(jnp.concatenate([v, other], 0), *before), "zh")
    far = both_ways(tie(near[:n], *between), "zh")
    got = swap(tie(jnp.concatenate([near, far], 0), *after))
    mine = by_block((v, near[:n], near[n:], far))
    theirs = by_block((other, got[:n], got[n : 2 * n], got[2 * n :]))
    return jnp.concatenate([mine, theirs], 0), near


def by_block(parts):
    n = parts[0].shape[0] // 8
    return jnp.stack([p.reshape(n, 8, ROWS) for p in parts], 1).reshape(32 * n, ROWS)


def gather_x(full, before=(), between=()):
    half = full.shape[0] // 2
    near = both_ways(tie(full, *before), "x")
    far = both_ways(tie(near[:half], *between), "x")
    return (full, near, far, swap(near), swap(far))


def chunks(n, i):
    return (i, n + i, 2 * n + i, 3 * n + i, 4 * n + i, 5 * n + i, 6 * n + i, 7 * n + i)


def column_order(ring):
    z, x, c = (lax.axis_index(a) for a in COL)
    s = 1 - 2 * c

    def half(core, sign):
        if ring:
            return [(z, core), (z - sign, core), (z - sign, 1 - core), (z + 2, core)]
        return [(i, core) for i in range(4)]

    mine, theirs = half(c, s), half(1 - c, -s)
    order = [(x, mine), (x, theirs), (x - s, mine), (x - s, theirs), (x + 2, mine)]
    order += [(x + s, theirs), (x + s, mine), (x + 2, theirs)]
    unit = jnp.stack([((zz % 4) * 4 + xx % 4) * 2 + cc for xx, units in order for zz, cc in units])
    return (unit[:, None] * 8 + jnp.arange(8)[None, :]).reshape(NB)


def exchange(eigvecs):
    return lax.all_to_all(eigvecs.T.reshape(32, K, 128), COL, split_axis=0, concat_axis=0, tiled=True)


def row_share(a):
    n, width = a.shape
    a = lax.all_to_all(a.reshape(8, n // 8, width), ROW, split_axis=0, concat_axis=0, tiled=True)
    return jnp.sum(a, 0)


def hand_on(share):
    n, width = share.shape
    a = jnp.broadcast_to(share, (8, n, width))
    return lax.all_to_all(a, ROW, split_axis=0, concat_axis=0, tiled=True).reshape(8 * n, width)


def row_sum_small(w):
    w = w + shift(w, "zl", 1)
    return w + shift(w, "y", 1) + shift(w, "y", 2) + shift(w, "y", 3)


def split(a):
    hi = a.astype(jnp.bfloat16)
    return hi, (a - hi.astype(jnp.float32)).astype(jnp.bfloat16)


def dot(a, b, dims):
    return lax.dot_general(a, b, (dims, ((), ())), preferred_element_type=jnp.float32)


NT = ((1,), (1,))
NN = ((1,), (0,))


def project(v, cur):
    (vh, vl), (ch, cl) = v, cur
    n = ch.shape[0]
    both = dot(vh, jnp.concatenate([ch, cl], 0), NT)
    return both[:, :n] + both[:, n:] + dot(vl, ch, NT)


def spread_out(applied, v):
    (ah, al), (vh, vl) = applied, v
    both = dot(jnp.concatenate([ah, al], 0), vh, NN)
    return both[:K] + both[K:] + dot(ah, vl, NN)


def stacked(refs):
    return jnp.concatenate([r[...] for r in refs], 0)


def block_of(a, i, n):
    return jnp.concatenate([a[32 * k : 32 * k + 32] for k in chunks(n, i)], 0)


def work_kernel(has_old, has_new, *refs):
    cur_ref, refs = refs[0], refs[1:]
    cur = cur_ref[...] if len(cur_ref.shape) == 2 else jnp.concatenate([cur_ref[i] for i in range(STEP // 128)], 1)
    if has_old:
        applied, old, refs = split(refs[0][...]), split(stacked(refs[1:6])), refs[6:]
        cur = cur - spread_out(applied, old)
    if not has_new:
        refs[0][...] = cur.T
        return
    new, refs = stacked(refs[:5]), refs[5:]
    if has_old:
        refs[0][...] = cur
        refs = refs[1:]
    w_ref = refs[0]
    if new.shape[0] == NB:
        part = project(split(new), split(cur))
    else:
        high, low = split(new)
        first, second = ((block_of(high, i, 2), block_of(low, i, 2)) for i in range(2))
        now = split(cur)
        g = project(second, first)
        part = jnp.concatenate([project(first, now), project(second, now), g[:, :K], g[:, K:]], 0)

    @pl.when(pl.program_id(0) == 0)
    def _():
        w_ref[...] = part

    @pl.when(pl.program_id(0) != 0)
    def _():
        w_ref[...] += part


def piece_specs(pieces):
    return [pl.BlockSpec((p.shape[0], STEP), lambda i: (0, i)) for p in pieces]


def rows_of(pieces):
    return sum(p.shape[0] for p in pieces)


def work(cur, applied, old, new):
    args, specs = [cur], [pl.BlockSpec((K, STEP), lambda i: (0, i))]
    if cur.ndim == 3:
        specs = [pl.BlockSpec((STEP // 128, K, 128), lambda i: (i, 0, 0))]
    if old:
        args += [applied, *old]
        specs += [pl.BlockSpec(applied.shape, lambda i: (0, 0))] + piece_specs(old)
    args += new
    specs += piece_specs(new)
    shapes, outs = [], []
    if not new:
        shapes.append(jax.ShapeDtypeStruct((ROWS, K), jnp.float32))
        outs.append(pl.BlockSpec((STEP, K), lambda i: (i, 0)))
    elif old:
        shapes.append(jax.ShapeDtypeStruct((K, ROWS), jnp.float32))
        outs.append(pl.BlockSpec((K, STEP), lambda i: (0, i)))
    if new:
        n = 1024 if rows_of(new) > NB else NB
        shapes.append(jax.ShapeDtypeStruct((n, K), jnp.float32))
        outs.append(pl.BlockSpec((n, K), lambda i: (0, 0)))
    n = rows_of(old) + rows_of(new)
    return pl.pallas_call(
        functools.partial(work_kernel, bool(old), bool(new)),
        grid=(ROWS // STEP,),
        in_specs=specs,
        out_specs=outs,
        out_shape=shapes,
        compiler_params=pltpu.CompilerParams(vmem_limit_bytes=50 << 20),
        cost_estimate=pl.CostEstimate(
            flops=6 * n * K * ROWS, bytes_accessed=4 * ROWS * (n + 2 * K), transcendentals=0
        ),
        name="work",
    )(*args)


def exact(a, b):
    return lax.dot_general(a, b, (NN, ((), ())), precision=HIGHEST, preferred_element_type=jnp.float32)


def solve_kernel(n, t_ref, w_ref, out):
    done = [exact(t_ref[0], w_ref[:NB])]
    if n == 2:
        g = exact(w_ref[2 * NB : 3 * NB], done[0][:K]) + exact(w_ref[3 * NB :], done[0][K:])
        done.append(exact(t_ref[1], w_ref[NB : 2 * NB] - g))
    laid = sorted((k, i, j) for i in range(n) for j, k in enumerate(chunks(n, i)))
    out[...] = jnp.concatenate([done[i][32 * j : 32 * j + 32] for _, i, j in laid], 0).T


def solve(t, w):
    n = t.shape[0]
    return pl.pallas_call(
        functools.partial(solve_kernel, n),
        out_shape=jax.ShapeDtypeStruct((K, NB * n), jnp.float32),
        cost_estimate=pl.CostEstimate(flops=12 * n * NB * NB * K, bytes_accessed=1 << 20, transcendentals=0),
        compiler_params=pltpu.CompilerParams(vmem_limit_bytes=24 << 20),
        name="solve",
    )(t, w)


def on_device(eigvecs, householder, tfactor):
    v = jnp.swapaxes(householder, 1, 2)

    v43, v21 = jnp.concatenate([v[4], v[3]], 0), jnp.concatenate([v[2], v[1]], 0)
    full43, _ = gather_z(v43, swap(v43))
    cur = exchange(eigvecs)
    pieces43 = gather_x(full43, (), (cur,))
    near43, far43 = pieces43[1:3]
    full21, _ = gather_z(v21, swap(v21), (full43,), (near43, cur), (far43,))
    (w,) = work(cur, None, (), pieces43)
    share = row_share(w)
    pieces21 = gather_x(full21, (far43,), (share,))
    near21, far21 = pieces21[1:3]
    full0, _ = gather_z(v[0], swap(v[0]), (far43,), (share,))
    pieces0 = gather_x(full0, (near21,), (far21,))

    def ordered(ring, *blocks):
        pick = (column_order(ring)[:, None] == jnp.arange(NB)[None, :]).astype(jnp.float32)
        part = jnp.stack([tfactor[b] for b in blocks])
        return jnp.einsum("ij,bjk,lk->bil", pick, part, pick, precision=HIGHEST)

    applied = solve(ordered(True, 4, 3), hand_on(share))
    cur, w = work(cur, applied, pieces43, pieces21)
    applied = solve(ordered(True, 2, 1), hand_on(row_share(w)))
    cur, w = work(cur, applied, pieces21, pieces0)
    applied = solve(ordered(True, 0), row_sum_small(w))
    return work(cur, applied, pieces0, ())[0]


def solution(mesh):
    fine = Mesh(mesh.devices.reshape(SIZES), AXES)
    placed = (P(ROW + COL, None), P(None, ROW, COL), P())
    return jax.shard_map(on_device, mesh=fine, in_specs=placed, out_specs=P(ROW, COL), check_vma=False)
```

```python
import functools

import jax
import jax.numpy as jnp
from jax import lax
from jax.experimental import pallas as pl
from jax.experimental.pallas import tpu as pltpu
from jax.sharding import Mesh
from jax.sharding import PartitionSpec as P

AXES = ("zl", "y", "zh", "x", "core")
SIZES = (2, 4, 4, 4, 2)
ROW, COL = ("zl", "y"), ("zh", "x", "core")
RING = 4
ROWS = 4096
NB = 256
K = 128
STEP = 1024
HIGHEST = lax.Precision.HIGHEST


def tie(a, *events):
    return lax.optimization_barrier((a, *events))[0] if events else a


def shift(a, axis, by):
    n = SIZES[AXES.index(axis)]
    return lax.ppermute(a, axis, [(i, (i + by) % n) for i in range(n)])


def both_ways(a, axis):
    pairs = []
    for i in range(RING):
        pairs.append((i * 2, ((i + 1) % RING) * 2))
        pairs.append((i * 2 + 1, ((i - 1) % RING) * 2 + 1))
    return lax.ppermute(a, (axis, "core"), pairs)


def swap(a):
    return shift(a, "core", 1)


def gather_z(v, other, before=(), between=(), after=()):
    n = v.shape[0]
    near = both_ways(tie(jnp.concatenate([v, other], 0), *before), "zh")
    far = both_ways(tie(near[:n], *between), "zh")
    got = swap(tie(jnp.concatenate([near, far], 0), *after))
    mine = by_block((v, near[:n], near[n:], far))
    theirs = by_block((other, got[:n], got[n : 2 * n], got[2 * n :]))
    return jnp.concatenate([mine, theirs], 0), near


def by_block(parts):
    n = parts[0].shape[0] // 8
    return jnp.stack([p.reshape(n, 8, ROWS) for p in parts], 1).reshape(32 * n, ROWS)


def gather_x(full, before=(), between=()):
    half = full.shape[0] // 2
    near = both_ways(tie(full, *before), "x")
    far = both_ways(tie(near[:half], *between), "x")
    return (full, near, far, swap(near), swap(far))


def chunks(n, i):
    return (i, n + i, 2 * n + i, 3 * n + i, 4 * n + i, 5 * n + i, 6 * n + i, 7 * n + i)


def column_order(ring):
    z, x, c = (lax.axis_index(a) for a in COL)
    s = 1 - 2 * c

    def half(core, sign):
        if ring:
            return [(z, core), (z - sign, core), (z - sign, 1 - core), (z + 2, core)]
        return [(i, core) for i in range(4)]

    mine, theirs = half(c, s), half(1 - c, -s)
    order = [(x, mine), (x, theirs), (x - s, mine), (x - s, theirs), (x + 2, mine)]
    order += [(x + s, theirs), (x + s, mine), (x + 2, theirs)]
    unit = jnp.stack([((zz % 4) * 4 + xx % 4) * 2 + cc for xx, units in order for zz, cc in units])
    return (unit[:, None] * 8 + jnp.arange(8)[None, :]).reshape(NB)


def exchange(eigvecs):
    return lax.all_to_all(eigvecs.T.reshape(32, K, 128), COL, split_axis=0, concat_axis=0, tiled=True)


def row_share(a):
    n, width = a.shape
    a = lax.all_to_all(a.reshape(8, n // 8, width), ROW, split_axis=0, concat_axis=0, tiled=True)
    return jnp.sum(a, 0)


def hand_on(share):
    n, width = share.shape
    a = jnp.broadcast_to(share, (8, n, width))
    return lax.all_to_all(a, ROW, split_axis=0, concat_axis=0, tiled=True).reshape(8 * n, width)


def row_sum_small(w):
    w = w + shift(w, "zl", 1)
    return w + shift(w, "y", 1) + shift(w, "y", 2) + shift(w, "y", 3)


def split(a):
    hi = a.astype(jnp.bfloat16)
    return hi, (a - hi.astype(jnp.float32)).astype(jnp.bfloat16)


def dot(a, b, dims):
    return lax.dot_general(a, b, (dims, ((), ())), preferred_element_type=jnp.float32)


NT = ((1,), (1,))
NN = ((1,), (0,))


def project(v, cur):
    (vh, vl), (ch, cl) = v, cur
    n = ch.shape[0]
    both = dot(vh, jnp.concatenate([ch, cl], 0), NT)
    return both[:, :n] + both[:, n:] + dot(vl, ch, NT)


def spread_out(applied, v):
    (ah, al), (vh, vl) = applied, v
    both = dot(jnp.concatenate([ah, al], 0), vh, NN)
    return both[:K] + both[K:] + dot(ah, vl, NN)


def stacked(refs):
    return jnp.concatenate([r[...] for r in refs], 0)


def block_of(a, i, n):
    return jnp.concatenate([a[32 * k : 32 * k + 32] for k in chunks(n, i)], 0)


def work_kernel(has_old, has_new, *refs):
    cur_ref, refs = refs[0], refs[1:]
    cur = cur_ref[...] if len(cur_ref.shape) == 2 else jnp.concatenate([cur_ref[i] for i in range(STEP // 128)], 1)
    if has_old:
        applied, old, refs = split(refs[0][...]), split(stacked(refs[1:6])), refs[6:]
        cur = cur - spread_out(applied, old)
    if not has_new:
        refs[0][...] = cur.T
        return
    new, refs = stacked(refs[:5]), refs[5:]
    if has_old:
        refs[0][...] = cur
        refs = refs[1:]
    w_ref = refs[0]
    if new.shape[0] == NB:
        part = project(split(new), split(cur))
    else:
        high, low = split(new)
        first, second = ((block_of(high, i, 2), block_of(low, i, 2)) for i in range(2))
        now = split(cur)
        g = project(second, first)
        part = jnp.concatenate([project(first, now), project(second, now), g[:, :K], g[:, K:]], 0)

    @pl.when(pl.program_id(0) == 0)
    def _():
        w_ref[...] = part

    @pl.when(pl.program_id(0) != 0)
    def _():
        w_ref[...] += part


def piece_specs(pieces):
    return [pl.BlockSpec((p.shape[0], STEP), lambda i: (0, i)) for p in pieces]


def rows_of(pieces):
    return sum(p.shape[0] for p in pieces)


def work(cur, applied, old, new):
    args, specs = [cur], [pl.BlockSpec((K, STEP), lambda i: (0, i))]
    if cur.ndim == 3:
        specs = [pl.BlockSpec((STEP // 128, K, 128), lambda i: (i, 0, 0))]
    if old:
        args += [applied, *old]
        specs += [pl.BlockSpec(applied.shape, lambda i: (0, 0))] + piece_specs(old)
    args += new
    specs += piece_specs(new)
    shapes, outs = [], []
    if not new:
        shapes.append(jax.ShapeDtypeStruct((ROWS, K), jnp.float32))
        outs.append(pl.BlockSpec((STEP, K), lambda i: (i, 0)))
    elif old:
        shapes.append(jax.ShapeDtypeStruct((K, ROWS), jnp.float32))
        outs.append(pl.BlockSpec((K, STEP), lambda i: (0, i)))
    if new:
        n = 1024 if rows_of(new) > NB else NB
        shapes.append(jax.ShapeDtypeStruct((n, K), jnp.float32))
        outs.append(pl.BlockSpec((n, K), lambda i: (0, 0)))
    n = rows_of(old) + rows_of(new)
    return pl.pallas_call(
        functools.partial(work_kernel, bool(old), bool(new)),
        grid=(ROWS // STEP,),
        in_specs=specs,
        out_specs=outs,
        out_shape=shapes,
        compiler_params=pltpu.CompilerParams(vmem_limit_bytes=50 << 20),
        cost_estimate=pl.CostEstimate(
            flops=6 * n * K * ROWS, bytes_accessed=4 * ROWS * (n + 2 * K), transcendentals=0
        ),
        name="work",
    )(*args)


def exact(a, b):
    return lax.dot_general(a, b, (NN, ((), ())), precision=HIGHEST, preferred_element_type=jnp.float32)


def solve_kernel(n, t_ref, w_ref, out):
    done = [exact(t_ref[0], w_ref[:NB])]
    if n == 2:
        g = exact(w_ref[2 * NB : 3 * NB], done[0][:K]) + exact(w_ref[3 * NB :], done[0][K:])
        done.append(exact(t_ref[1], w_ref[NB : 2 * NB] - g))
    laid = sorted((k, i, j) for i in range(n) for j, k in enumerate(chunks(n, i)))
    out[...] = jnp.concatenate([done[i][32 * j : 32 * j + 32] for _, i, j in laid], 0).T


def solve(t, w):
    n = t.shape[0]
    return pl.pallas_call(
        functools.partial(solve_kernel, n),
        out_shape=jax.ShapeDtypeStruct((K, NB * n), jnp.float32),
        cost_estimate=pl.CostEstimate(flops=12 * n * NB * NB * K, bytes_accessed=1 << 20, transcendentals=0),
        compiler_params=pltpu.CompilerParams(vmem_limit_bytes=24 << 20),
        name="solve",
    )(t, w)


def on_device(eigvecs, householder, tfactor):
    v = jnp.swapaxes(householder, 1, 2)

    v43, v21 = jnp.concatenate([v[4], v[3]], 0), jnp.concatenate([v[2], v[1]], 0)
    full43, _ = gather_z(v43, swap(v43))
    cur = exchange(eigvecs)
    pieces43 = gather_x(full43, (), ())
    near43, far43 = pieces43[1:3]
    full21, _ = gather_z(v21, swap(v21), (full43,), (near43, cur), ())
    (w,) = work(cur, None, (), pieces43)
    share = row_share(w)
    pieces21 = gather_x(full21, (far43,), (share,))
    near21, far21 = pieces21[1:3]
    full0, _ = gather_z(v[0], swap(v[0]), (far43,), (share,))
    pieces0 = gather_x(full0, (near21,), (far21,))

    def ordered(ring, *blocks):
        pick = (column_order(ring)[:, None] == jnp.arange(NB)[None, :]).astype(jnp.float32)
        part = jnp.stack([tfactor[b] for b in blocks])
        return jnp.einsum("ij,bjk,lk->bil", pick, part, pick, precision=HIGHEST)

    applied = solve(ordered(True, 4, 3), hand_on(share))
    cur, w = work(cur, applied, pieces43, pieces21)
    applied = solve(ordered(True, 2, 1), hand_on(row_share(w)))
    cur, w = work(cur, applied, pieces21, pieces0)
    applied = solve(ordered(True, 0), row_sum_small(w))
    return work(cur, applied, pieces0, ())[0]


def solution(mesh):
    fine = Mesh(mesh.devices.reshape(SIZES), AXES)
    placed = (P(ROW + COL, None), P(None, ROW, COL), P())
    return jax.shard_map(on_device, mesh=fine, in_specs=placed, out_specs=P(ROW, COL), check_vma=False)
```

```python
import functools

import jax
import jax.numpy as jnp
from jax import lax
from jax.experimental import pallas as pl
from jax.experimental.pallas import tpu as pltpu
from jax.sharding import Mesh
from jax.sharding import PartitionSpec as P

AXES = ("zl", "y", "zh", "x", "core")
SIZES = (2, 4, 4, 4, 2)
ROW, COL = ("zl", "y"), ("zh", "x", "core")
RING = 4
ROWS = 4096
NB = 256
K = 128
STEP = 1024
PIECES = 8
HIGHEST = lax.Precision.HIGHEST


def tie(a, *events):
    return lax.optimization_barrier((a, *events))[0] if events else a


def shift(a, axis, by):
    n = SIZES[AXES.index(axis)]
    return lax.ppermute(a, axis, [(i, (i + by) % n) for i in range(n)])


def both_ways(a, axis):
    pairs = []
    for i in range(RING):
        pairs.append((i * 2, ((i + 1) % RING) * 2))
        pairs.append((i * 2 + 1, ((i - 1) % RING) * 2 + 1))
    return lax.ppermute(a, (axis, "core"), pairs)


def swap(a):
    return shift(a, "core", 1)


def gather_z(v, other, before=(), between=(), after=()):
    n = v.shape[0]
    near = both_ways(tie(jnp.concatenate([v, other], 0), *before), "zh")
    far = both_ways(tie(near[:n], *between), "zh")
    got = swap(tie(jnp.concatenate([near, far], 0), *after))
    mine = by_block((v, near[:n], near[n:], far))
    theirs = by_block((other, got[:n], got[n : 2 * n], got[2 * n :]))
    return mine, theirs


def by_block(parts):
    n = parts[0].shape[0] // 8
    return jnp.stack([p.reshape(n, 8, ROWS) for p in parts], 1).reshape(32 * n, ROWS)


def gather_x(mine, theirs, before=(), between=()):
    near = both_ways(tie(mine, *before), "x")
    near2 = both_ways(tie(theirs, *before), "x")
    far = both_ways(tie(near, *between), "x")
    return (mine, theirs, near, near2, far, swap(near), swap(near2), swap(far))


def chunks(n, i):
    return tuple(n * piece + i for piece in range(PIECES))


def column_order(ring):
    z, x, c = (lax.axis_index(a) for a in COL)
    s = 1 - 2 * c

    def half(core, sign):
        if ring:
            return [(z, core), (z - sign, core), (z - sign, 1 - core), (z + 2, core)]
        return [(i, core) for i in range(4)]

    mine, theirs = half(c, s), half(1 - c, -s)
    order = [(x, mine), (x, theirs), (x - s, mine), (x - s, theirs), (x + 2, mine)]
    order += [(x + s, theirs), (x + s, mine), (x + 2, theirs)]
    unit = jnp.stack([((zz % 4) * 4 + xx % 4) * 2 + cc for xx, units in order for zz, cc in units])
    return (unit[:, None] * 8 + jnp.arange(8)[None, :]).reshape(NB)


def exchange(eigvecs):
    return lax.all_to_all(eigvecs.T.reshape(32, K, 128), COL, split_axis=0, concat_axis=0, tiled=True)


def row_share(a):
    n, width = a.shape
    a = lax.all_to_all(a.reshape(8, n // 8, width), ROW, split_axis=0, concat_axis=0, tiled=True)
    return jnp.sum(a, 0)


def hand_on(share):
    n, width = share.shape
    a = jnp.broadcast_to(share, (8, n, width))
    return lax.all_to_all(a, ROW, split_axis=0, concat_axis=0, tiled=True).reshape(8 * n, width)


def row_sum_small(w):
    w = w + shift(w, "zl", 1)
    return w + shift(w, "y", 1) + shift(w, "y", 2) + shift(w, "y", 3)


def split(a):
    hi = a.astype(jnp.bfloat16)
    return hi, (a - hi.astype(jnp.float32)).astype(jnp.bfloat16)


def dot(a, b, dims):
    return lax.dot_general(a, b, (dims, ((), ())), preferred_element_type=jnp.float32)


NT = ((1,), (1,))
NN = ((1,), (0,))


def project(v, cur):
    (vh, vl), (ch, cl) = v, cur
    n = ch.shape[0]
    both = dot(vh, jnp.concatenate([ch, cl], 0), NT)
    return both[:, :n] + both[:, n:] + dot(vl, ch, NT)


def spread_out(applied, v):
    (ah, al), (vh, vl) = applied, v
    both = dot(jnp.concatenate([ah, al], 0), vh, NN)
    return both[:K] + both[K:] + dot(ah, vl, NN)


def stacked(refs):
    return jnp.concatenate([r[...] for r in refs], 0)


def block_of(a, i, n):
    return jnp.concatenate([a[32 * k : 32 * k + 32] for k in chunks(n, i)], 0)


def work_kernel(has_old, has_new, *refs):
    cur_ref, refs = refs[0], refs[1:]
    cur = cur_ref[...] if len(cur_ref.shape) == 2 else jnp.concatenate([cur_ref[i] for i in range(STEP // 128)], 1)
    if has_old:
        applied, old, refs = split(refs[0][...]), split(stacked(refs[1 : 1 + PIECES])), refs[1 + PIECES :]
        cur = cur - spread_out(applied, old)
    if not has_new:
        refs[0][...] = cur.T
        return
    new, refs = stacked(refs[:PIECES]), refs[PIECES:]
    if has_old:
        refs[0][...] = cur
        refs = refs[1:]
    w_ref = refs[0]
    if new.shape[0] == NB:
        part = project(split(new), split(cur))
    else:
        high, low = split(new)
        first, second = ((block_of(high, i, 2), block_of(low, i, 2)) for i in range(2))
        now = split(cur)
        g = project(second, first)
        part = jnp.concatenate([project(first, now), project(second, now), g[:, :K], g[:, K:]], 0)

    @pl.when(pl.program_id(0) == 0)
    def _():
        w_ref[...] = part

    @pl.when(pl.program_id(0) != 0)
    def _():
        w_ref[...] += part


def piece_specs(pieces):
    return [pl.BlockSpec((p.shape[0], STEP), lambda i: (0, i)) for p in pieces]


def rows_of(pieces):
    return sum(p.shape[0] for p in pieces)


def work(cur, applied, old, new):
    args, specs = [cur], [pl.BlockSpec((K, STEP), lambda i: (0, i))]
    if cur.ndim == 3:
        specs = [pl.BlockSpec((STEP // 128, K, 128), lambda i: (i, 0, 0))]
    if old:
        args += [applied, *old]
        specs += [pl.BlockSpec(applied.shape, lambda i: (0, 0))] + piece_specs(old)
    args += new
    specs += piece_specs(new)
    shapes, outs = [], []
    if not new:
        shapes.append(jax.ShapeDtypeStruct((ROWS, K), jnp.float32))
        outs.append(pl.BlockSpec((STEP, K), lambda i: (i, 0)))
    elif old:
        shapes.append(jax.ShapeDtypeStruct((K, ROWS), jnp.float32))
        outs.append(pl.BlockSpec((K, STEP), lambda i: (0, i)))
    if new:
        n = 1024 if rows_of(new) > NB else NB
        shapes.append(jax.ShapeDtypeStruct((n, K), jnp.float32))
        outs.append(pl.BlockSpec((n, K), lambda i: (0, 0)))
    n = rows_of(old) + rows_of(new)
    return pl.pallas_call(
        functools.partial(work_kernel, bool(old), bool(new)),
        grid=(ROWS // STEP,),
        in_specs=specs,
        out_specs=outs,
        out_shape=shapes,
        compiler_params=pltpu.CompilerParams(vmem_limit_bytes=50 << 20),
        cost_estimate=pl.CostEstimate(
            flops=6 * n * K * ROWS, bytes_accessed=4 * ROWS * (n + 2 * K), transcendentals=0
        ),
        name="work",
    )(*args)


def exact(a, b):
    return lax.dot_general(a, b, (NN, ((), ())), precision=HIGHEST, preferred_element_type=jnp.float32)


def solve_kernel(n, t_ref, w_ref, out):
    done = [exact(t_ref[0], w_ref[:NB])]
    if n == 2:
        g = exact(w_ref[2 * NB : 3 * NB], done[0][:K]) + exact(w_ref[3 * NB :], done[0][K:])
        done.append(exact(t_ref[1], w_ref[NB : 2 * NB] - g))
    laid = sorted((k, i, j) for i in range(n) for j, k in enumerate(chunks(n, i)))
    out[...] = jnp.concatenate([done[i][32 * j : 32 * j + 32] for _, i, j in laid], 0).T


def solve(t, w):
    n = t.shape[0]
    return pl.pallas_call(
        functools.partial(solve_kernel, n),
        out_shape=jax.ShapeDtypeStruct((K, NB * n), jnp.float32),
        cost_estimate=pl.CostEstimate(flops=12 * n * NB * NB * K, bytes_accessed=1 << 20, transcendentals=0),
        compiler_params=pltpu.CompilerParams(vmem_limit_bytes=24 << 20),
        name="solve",
    )(t, w)


def on_device(eigvecs, householder, tfactor):
    v = jnp.swapaxes(householder, 1, 2)

    v43, v21 = jnp.concatenate([v[4], v[3]], 0), jnp.concatenate([v[2], v[1]], 0)
    ring43 = gather_z(v43, swap(v43))
    cur = exchange(eigvecs)
    pieces43 = gather_x(*ring43)
    near43, far43 = pieces43[2], pieces43[4]
    ring21 = gather_z(v21, swap(v21), (near43,cur), (), ())
    (w,) = work(cur, None, (), pieces43)
    share = row_share(w)
    pieces21 = gather_x(*ring21, (far43,), (share,))
    near21, far21 = pieces21[3], pieces21[4]
    ring0 = gather_z(v[0], swap(v[0]), (far43,), (share,))
    pieces0 = gather_x(*ring0, (near21,), (far21,))

    def ordered(ring, *blocks):
        pick = (column_order(ring)[:, None] == jnp.arange(NB)[None, :]).astype(jnp.float32)
        part = jnp.stack([tfactor[b] for b in blocks])
        return jnp.einsum("ij,bjk,lk->bil", pick, part, pick, precision=HIGHEST)

    applied = solve(ordered(True, 4, 3), hand_on(share))
    cur, w = work(cur, applied, pieces43, pieces21)
    applied = solve(ordered(True, 2, 1), hand_on(row_share(w)))
    cur, w = work(cur, applied, pieces21, pieces0)
    applied = solve(ordered(True, 0), row_sum_small(w))
    return work(cur, applied, pieces0, ())[0]


def solution(mesh):
    fine = Mesh(mesh.devices.reshape(SIZES), AXES)
    placed = (P(ROW + COL, None), P(None, ROW, COL), P())
    return jax.shard_map(on_device, mesh=fine, in_specs=placed, out_specs=P(ROW, COL), check_vma=False)
```

```python
import functools

import jax
import jax.numpy as jnp
from jax import lax
from jax.experimental import pallas as pl
from jax.experimental.pallas import tpu as pltpu
from jax.sharding import Mesh
from jax.sharding import PartitionSpec as P

AXES = ("zl", "y", "zh", "x", "core")
SIZES = (2, 4, 4, 4, 2)
ROW, COL = ("zl", "y"), ("zh", "x", "core")
RING = 4
ROWS = 4096
NB = 256
K = 128
STEP = 1024
PIECES = 8
HIGHEST = lax.Precision.HIGHEST


def tie(a, *events):
    return lax.optimization_barrier((a, *events))[0] if events else a


def shift(a, axis, by):
    n = SIZES[AXES.index(axis)]
    return lax.ppermute(a, axis, [(i, (i + by) % n) for i in range(n)])


def both_ways(a, axis):
    pairs = []
    for i in range(RING):
        pairs.append((i * 2, ((i + 1) % RING) * 2))
        pairs.append((i * 2 + 1, ((i - 1) % RING) * 2 + 1))
    return lax.ppermute(a, (axis, "core"), pairs)


def swap(a):
    return shift(a, "core", 1)


def gather_z(v, other, before=(), between=(), after=()):
    n = v.shape[0]
    near = both_ways(tie(jnp.concatenate([v, other], 0), *before), "zh")
    far = both_ways(tie(near[:n], *between), "zh")
    got = swap(tie(jnp.concatenate([near, far], 0), *after))
    mine = by_block((v, near[:n], near[n:], far))
    theirs = by_block((other, got[:n], got[n : 2 * n], got[2 * n :]))
    return mine, theirs


def by_block(parts):
    n = parts[0].shape[0] // 8
    return jnp.stack([p.reshape(n, 8, ROWS) for p in parts], 1).reshape(32 * n, ROWS)


def gather_x(mine, theirs, before=(), between=(), after=()):
    near = both_ways(tie(mine, *before), "x")
    near2 = both_ways(tie(theirs, *before), "x")
    far = both_ways(tie(near, *between), "x")
    return (mine, theirs, near, near2, far, swap(near), swap(tie(near2, *after)), swap(tie(far, *after)))


def chunks(n, i):
    return tuple(n * piece + i for piece in range(PIECES))


def column_order(ring):
    z, x, c = (lax.axis_index(a) for a in COL)
    s = 1 - 2 * c

    def half(core, sign):
        if ring:
            return [(z, core), (z - sign, core), (z - sign, 1 - core), (z + 2, core)]
        return [(i, core) for i in range(4)]

    mine, theirs = half(c, s), half(1 - c, -s)
    order = [(x, mine), (x, theirs), (x - s, mine), (x - s, theirs), (x + 2, mine)]
    order += [(x + s, theirs), (x + s, mine), (x + 2, theirs)]
    unit = jnp.stack([((zz % 4) * 4 + xx % 4) * 2 + cc for xx, units in order for zz, cc in units])
    return (unit[:, None] * 8 + jnp.arange(8)[None, :]).reshape(NB)


def exchange(eigvecs):
    return lax.all_to_all(eigvecs.T.reshape(32, K, 128), COL, split_axis=0, concat_axis=0, tiled=True)


def row_share(a):
    n, width = a.shape
    a = lax.all_to_all(a.reshape(8, n // 8, width), ROW, split_axis=0, concat_axis=0, tiled=True)
    return jnp.sum(a, 0)


def hand_on(share):
    n, width = share.shape
    a = jnp.broadcast_to(share, (8, n, width))
    return lax.all_to_all(a, ROW, split_axis=0, concat_axis=0, tiled=True).reshape(8 * n, width)


def row_sum_small(w):
    w = w + shift(w, "zl", 1)
    return w + shift(w, "y", 1) + shift(w, "y", 2) + shift(w, "y", 3)


def split(a):
    hi = a.astype(jnp.bfloat16)
    return hi, (a - hi.astype(jnp.float32)).astype(jnp.bfloat16)


def dot(a, b, dims):
    return lax.dot_general(a, b, (dims, ((), ())), preferred_element_type=jnp.float32)


NT = ((1,), (1,))
NN = ((1,), (0,))


def project(v, cur):
    (vh, vl), (ch, cl) = v, cur
    n = ch.shape[0]
    both = dot(vh, jnp.concatenate([ch, cl], 0), NT)
    return both[:, :n] + both[:, n:] + dot(vl, ch, NT)


def spread_out(applied, v):
    (ah, al), (vh, vl) = applied, v
    both = dot(jnp.concatenate([ah, al], 0), vh, NN)
    return both[:K] + both[K:] + dot(ah, vl, NN)


def stacked(refs):
    return jnp.concatenate([r[...] for r in refs], 0)


def block_of(a, i, n):
    return jnp.concatenate([a[32 * k : 32 * k + 32] for k in chunks(n, i)], 0)


def work_kernel(has_old, has_new, *refs):
    cur_ref, refs = refs[0], refs[1:]
    cur = cur_ref[...] if len(cur_ref.shape) == 2 else jnp.concatenate([cur_ref[i] for i in range(STEP // 128)], 1)
    if has_old:
        applied, old, refs = split(refs[0][...]), split(stacked(refs[1 : 1 + PIECES])), refs[1 + PIECES :]
        cur = cur - spread_out(applied, old)
    if not has_new:
        refs[0][...] = cur.T
        return
    new, refs = stacked(refs[:PIECES]), refs[PIECES:]
    if has_old:
        refs[0][...] = cur
        refs = refs[1:]
    w_ref = refs[0]
    if new.shape[0] == NB:
        part = project(split(new), split(cur))
    else:
        high, low = split(new)
        first, second = ((block_of(high, i, 2), block_of(low, i, 2)) for i in range(2))
        now = split(cur)
        g = project(second, first)
        part = jnp.concatenate([project(first, now), project(second, now), g[:, :K], g[:, K:]], 0)

    @pl.when(pl.program_id(0) == 0)
    def _():
        w_ref[...] = part

    @pl.when(pl.program_id(0) != 0)
    def _():
        w_ref[...] += part


def piece_specs(pieces):
    return [pl.BlockSpec((p.shape[0], STEP), lambda i: (0, i)) for p in pieces]


def rows_of(pieces):
    return sum(p.shape[0] for p in pieces)


def work(cur, applied, old, new):
    args, specs = [cur], [pl.BlockSpec((K, STEP), lambda i: (0, i))]
    if cur.ndim == 3:
        specs = [pl.BlockSpec((STEP // 128, K, 128), lambda i: (i, 0, 0))]
    if old:
        args += [applied, *old]
        specs += [pl.BlockSpec(applied.shape, lambda i: (0, 0))] + piece_specs(old)
    args += new
    specs += piece_specs(new)
    shapes, outs = [], []
    if not new:
        shapes.append(jax.ShapeDtypeStruct((ROWS, K), jnp.float32))
        outs.append(pl.BlockSpec((STEP, K), lambda i: (i, 0)))
    elif old:
        shapes.append(jax.ShapeDtypeStruct((K, ROWS), jnp.float32))
        outs.append(pl.BlockSpec((K, STEP), lambda i: (0, i)))
    if new:
        n = 1024 if rows_of(new) > NB else NB
        shapes.append(jax.ShapeDtypeStruct((n, K), jnp.float32))
        outs.append(pl.BlockSpec((n, K), lambda i: (0, 0)))
    n = rows_of(old) + rows_of(new)
    return pl.pallas_call(
        functools.partial(work_kernel, bool(old), bool(new)),
        grid=(ROWS // STEP,),
        in_specs=specs,
        out_specs=outs,
        out_shape=shapes,
        compiler_params=pltpu.CompilerParams(vmem_limit_bytes=50 << 20),
        cost_estimate=pl.CostEstimate(
            flops=6 * n * K * ROWS, bytes_accessed=4 * ROWS * (n + 2 * K), transcendentals=0
        ),
        name="work",
    )(*args)


def exact(a, b):
    return lax.dot_general(a, b, (NN, ((), ())), precision=HIGHEST, preferred_element_type=jnp.float32)


def solve_kernel(n, t_ref, w_ref, out):
    done = [exact(t_ref[0], w_ref[:NB])]
    if n == 2:
        g = exact(w_ref[2 * NB : 3 * NB], done[0][:K]) + exact(w_ref[3 * NB :], done[0][K:])
        done.append(exact(t_ref[1], w_ref[NB : 2 * NB] - g))
    laid = sorted((k, i, j) for i in range(n) for j, k in enumerate(chunks(n, i)))
    out[...] = jnp.concatenate([done[i][32 * j : 32 * j + 32] for _, i, j in laid], 0).T


def solve(t, w):
    n = t.shape[0]
    return pl.pallas_call(
        functools.partial(solve_kernel, n),
        out_shape=jax.ShapeDtypeStruct((K, NB * n), jnp.float32),
        cost_estimate=pl.CostEstimate(flops=12 * n * NB * NB * K, bytes_accessed=1 << 20, transcendentals=0),
        compiler_params=pltpu.CompilerParams(vmem_limit_bytes=24 << 20),
        name="solve",
    )(t, w)


def on_device(eigvecs, householder, tfactor):
    v = jnp.swapaxes(householder, 1, 2)

    v43, v21 = jnp.concatenate([v[4], v[3]], 0), jnp.concatenate([v[2], v[1]], 0)
    ring43 = gather_z(v43, swap(v43))
    cur = exchange(eigvecs)
    pieces43 = gather_x(*ring43)
    near43, far43 = pieces43[2], pieces43[4]
    ring21 = gather_z(v21, swap(v21), (ring43[1],), (near43, cur), ())
    (w,) = work(cur, None, (), pieces43)
    share = row_share(w)
    total = hand_on(share)
    pieces21 = gather_x(*ring21, (far43,), (), (total,))
    near21, far21 = pieces21[3], pieces21[4]
    ring0 = gather_z(v[0], swap(v[0]), (far43,), (total,))
    pieces0 = gather_x(*ring0, (near21,), (far21,))

    def ordered(ring, *blocks):
        pick = (column_order(ring)[:, None] == jnp.arange(NB)[None, :]).astype(jnp.float32)
        part = jnp.stack([tfactor[b] for b in blocks])
        return jnp.einsum("ij,bjk,lk->bil", pick, part, pick, precision=HIGHEST)

    applied = solve(ordered(True, 4, 3), total)
    cur, w = work(cur, applied, pieces43, pieces21)
    applied = solve(ordered(True, 2, 1), hand_on(row_share(w)))
    cur, w = work(cur, applied, pieces21, pieces0)
    applied = solve(ordered(True, 0), row_sum_small(w))
    return work(cur, applied, pieces0, ())[0]


def solution(mesh):
    fine = Mesh(mesh.devices.reshape(SIZES), AXES)
    placed = (P(ROW + COL, None), P(None, ROW, COL), P())
    return jax.shard_map(on_device, mesh=fine, in_specs=placed, out_specs=P(ROW, COL), check_vma=False)
```

```python
import functools

import jax
import jax.numpy as jnp
from jax import lax
from jax.experimental import pallas as pl
from jax.experimental.pallas import tpu as pltpu
from jax.sharding import Mesh
from jax.sharding import PartitionSpec as P

AXES = ("zl", "y", "zh", "x", "core")
SIZES = (2, 4, 4, 4, 2)
ROW, COL = ("zl", "y"), ("zh", "x", "core")
RING = 4
ROWS = 4096
NB = 256
K = 128
STEP = 1024
PIECES = 8
HIGHEST = lax.Precision.HIGHEST


def tie(a, *events):
    return lax.optimization_barrier((a, *events))[0] if events else a


def shift(a, axis, by):
    n = SIZES[AXES.index(axis)]
    return lax.ppermute(a, axis, [(i, (i + by) % n) for i in range(n)])


def both_ways(a, axis):
    pairs = []
    for i in range(RING):
        pairs.append((i * 2, ((i + 1) % RING) * 2))
        pairs.append((i * 2 + 1, ((i - 1) % RING) * 2 + 1))
    return lax.ppermute(a, (axis, "core"), pairs)


def swap(a):
    return shift(a, "core", 1)


def gather_z(v, other, before=(), between=(), after=()):
    n = v.shape[0]
    near = both_ways(tie(jnp.concatenate([v, other], 0), *before), "zh")
    far = both_ways(tie(near[:n], *between), "zh")
    got = swap(tie(jnp.concatenate([near, far], 0), *after))
    mine = by_block((v, near[:n], near[n:], far))
    theirs = by_block((other, got[:n], got[n : 2 * n], got[2 * n :]))
    return mine, theirs, near


def by_block(parts):
    n = parts[0].shape[0] // 8
    return jnp.stack([p.reshape(n, 8, ROWS) for p in parts], 1).reshape(32 * n, ROWS)


def gather_x(mine, theirs, before=(), between=(), after=()):
    near = both_ways(tie(mine, *before), "x")
    near2 = both_ways(tie(theirs, *before), "x")
    far = both_ways(tie(near, *between), "x")
    return (mine, theirs, near, near2, far, swap(near), swap(tie(near2, *after)), swap(tie(far, *after)))


def chunks(n, i):
    return tuple(n * piece + i for piece in range(PIECES))


def column_order(ring):
    z, x, c = (lax.axis_index(a) for a in COL)
    s = 1 - 2 * c

    def half(core, sign):
        if ring:
            return [(z, core), (z - sign, core), (z - sign, 1 - core), (z + 2, core)]
        return [(i, core) for i in range(4)]

    mine, theirs = half(c, s), half(1 - c, -s)
    order = [(x, mine), (x, theirs), (x - s, mine), (x - s, theirs), (x + 2, mine)]
    order += [(x + s, theirs), (x + s, mine), (x + 2, theirs)]
    unit = jnp.stack([((zz % 4) * 4 + xx % 4) * 2 + cc for xx, units in order for zz, cc in units])
    return (unit[:, None] * 8 + jnp.arange(8)[None, :]).reshape(NB)


def exchange(eigvecs):
    return lax.all_to_all(eigvecs.T.reshape(32, K, 128), COL, split_axis=0, concat_axis=0, tiled=True)


def row_share(a):
    n, width = a.shape
    a = lax.all_to_all(a.reshape(8, n // 8, width), ROW, split_axis=0, concat_axis=0, tiled=True)
    return jnp.sum(a, 0)


def hand_on(share):
    n, width = share.shape
    a = jnp.broadcast_to(share, (8, n, width))
    return lax.all_to_all(a, ROW, split_axis=0, concat_axis=0, tiled=True).reshape(8 * n, width)


def row_sum_small(w):
    w = w + shift(w, "zl", 1)
    return w + shift(w, "y", 1) + shift(w, "y", 2) + shift(w, "y", 3)


def split(a):
    hi = a.astype(jnp.bfloat16)
    return hi, (a - hi.astype(jnp.float32)).astype(jnp.bfloat16)


def dot(a, b, dims):
    return lax.dot_general(a, b, (dims, ((), ())), preferred_element_type=jnp.float32)


NT = ((1,), (1,))
NN = ((1,), (0,))


def project(v, cur):
    (vh, vl), (ch, cl) = v, cur
    n = ch.shape[0]
    both = dot(vh, jnp.concatenate([ch, cl], 0), NT)
    return both[:, :n] + both[:, n:] + dot(vl, ch, NT)


def spread_out(applied, v):
    (ah, al), (vh, vl) = applied, v
    both = dot(jnp.concatenate([ah, al], 0), vh, NN)
    return both[:K] + both[K:] + dot(ah, vl, NN)


def stacked(refs):
    return jnp.concatenate([r[...] for r in refs], 0)


def block_of(a, i, n):
    return jnp.concatenate([a[32 * k : 32 * k + 32] for k in chunks(n, i)], 0)


def work_kernel(has_old, has_new, *refs):
    cur_ref, refs = refs[0], refs[1:]
    cur = cur_ref[...] if len(cur_ref.shape) == 2 else jnp.concatenate([cur_ref[i] for i in range(STEP // 128)], 1)
    if has_old:
        applied, old, refs = split(refs[0][...]), split(stacked(refs[1 : 1 + PIECES])), refs[1 + PIECES :]
        cur = cur - spread_out(applied, old)
    if not has_new:
        refs[0][...] = cur.T
        return
    new, refs = stacked(refs[:PIECES]), refs[PIECES:]
    if has_old:
        refs[0][...] = cur
        refs = refs[1:]
    w_ref = refs[0]
    if new.shape[0] == NB:
        part = project(split(new), split(cur))
    else:
        high, low = split(new)
        first, second = ((block_of(high, i, 2), block_of(low, i, 2)) for i in range(2))
        now = split(cur)
        g = project(second, first)
        part = jnp.concatenate([project(first, now), project(second, now), g[:, :K], g[:, K:]], 0)

    @pl.when(pl.program_id(0) == 0)
    def _():
        w_ref[...] = part

    @pl.when(pl.program_id(0) != 0)
    def _():
        w_ref[...] += part


def piece_specs(pieces):
    return [pl.BlockSpec((p.shape[0], STEP), lambda i: (0, i)) for p in pieces]


def rows_of(pieces):
    return sum(p.shape[0] for p in pieces)


def work(cur, applied, old, new):
    args, specs = [cur], [pl.BlockSpec((K, STEP), lambda i: (0, i))]
    if cur.ndim == 3:
        specs = [pl.BlockSpec((STEP // 128, K, 128), lambda i: (i, 0, 0))]
    if old:
        args += [applied, *old]
        specs += [pl.BlockSpec(applied.shape, lambda i: (0, 0))] + piece_specs(old)
    args += new
    specs += piece_specs(new)
    shapes, outs = [], []
    if not new:
        shapes.append(jax.ShapeDtypeStruct((ROWS, K), jnp.float32))
        outs.append(pl.BlockSpec((STEP, K), lambda i: (i, 0)))
    elif old:
        shapes.append(jax.ShapeDtypeStruct((K, ROWS), jnp.float32))
        outs.append(pl.BlockSpec((K, STEP), lambda i: (0, i)))
    if new:
        n = 1024 if rows_of(new) > NB else NB
        shapes.append(jax.ShapeDtypeStruct((n, K), jnp.float32))
        outs.append(pl.BlockSpec((n, K), lambda i: (0, 0)))
    n = rows_of(old) + rows_of(new)
    return pl.pallas_call(
        functools.partial(work_kernel, bool(old), bool(new)),
        grid=(ROWS // STEP,),
        in_specs=specs,
        out_specs=outs,
        out_shape=shapes,
        compiler_params=pltpu.CompilerParams(vmem_limit_bytes=50 << 20),
        cost_estimate=pl.CostEstimate(
            flops=6 * n * K * ROWS, bytes_accessed=4 * ROWS * (n + 2 * K), transcendentals=0
        ),
        name="work",
    )(*args)


def exact(a, b):
    return lax.dot_general(a, b, (NN, ((), ())), precision=HIGHEST, preferred_element_type=jnp.float32)


def solve_kernel(n, t_ref, w_ref, out):
    done = [exact(t_ref[0], w_ref[:NB])]
    if n == 2:
        g = exact(w_ref[2 * NB : 3 * NB], done[0][:K]) + exact(w_ref[3 * NB :], done[0][K:])
        done.append(exact(t_ref[1], w_ref[NB : 2 * NB] - g))
    laid = sorted((k, i, j) for i in range(n) for j, k in enumerate(chunks(n, i)))
    out[...] = jnp.concatenate([done[i][32 * j : 32 * j + 32] for _, i, j in laid], 0).T


def solve(t, w):
    n = t.shape[0]
    return pl.pallas_call(
        functools.partial(solve_kernel, n),
        out_shape=jax.ShapeDtypeStruct((K, NB * n), jnp.float32),
        cost_estimate=pl.CostEstimate(flops=12 * n * NB * NB * K, bytes_accessed=1 << 20, transcendentals=0),
        compiler_params=pltpu.CompilerParams(vmem_limit_bytes=24 << 20),
        name="solve",
    )(t, w)


def on_device(eigvecs, householder, tfactor):
    v = jnp.swapaxes(householder, 1, 2)

    v43, v21 = jnp.concatenate([v[4], v[3]], 0), jnp.concatenate([v[2], v[1]], 0)
    ring43 = gather_z(v43, swap(v43))
    cur = exchange(tie(eigvecs, ring43[2]))
    mine, theirs, _ = ring43
    near43, other43 = both_ways(mine, "x"), both_ways(theirs, "x")
    far43 = both_ways(near43, "x")
    ring21 = gather_z(v21, swap(v21), (theirs,), (near43, cur), ())
    pieces43 = (mine, theirs, near43, other43, far43, swap(near43), swap(other43), swap(tie(far43, ring21[0])))
    (w,) = work(cur, None, (), pieces43)
    share = row_share(w)
    total = hand_on(share)
    pieces21 = gather_x(*ring21[:2], (far43,), (), (total,))
    near21, far21 = pieces21[3], pieces21[4]
    ring0 = gather_z(v[0], swap(v[0]), (far43,), (total,))
    pieces0 = gather_x(*ring0[:2], (near21,), (far21,))

    def ordered(ring, *blocks):
        pick = (column_order(ring)[:, None] == jnp.arange(NB)[None, :]).astype(jnp.float32)
        part = jnp.stack([tfactor[b] for b in blocks])
        return jnp.einsum("ij,bjk,lk->bil", pick, part, pick, precision=HIGHEST)

    applied = solve(ordered(True, 4, 3), total)
    cur, w = work(cur, applied, pieces43, pieces21)
    applied = solve(ordered(True, 2, 1), hand_on(row_share(w)))
    cur, w = work(cur, applied, pieces21, pieces0)
    applied = solve(ordered(True, 0), row_sum_small(w))
    return work(cur, applied, pieces0, ())[0]


def solution(mesh):
    fine = Mesh(mesh.devices.reshape(SIZES), AXES)
    placed = (P(ROW + COL, None), P(None, ROW, COL), P())
    return jax.shard_map(on_device, mesh=fine, in_specs=placed, out_specs=P(ROW, COL), check_vma=False)
```

```python
import functools

import jax
import jax.numpy as jnp
from jax import lax
from jax.experimental import pallas as pl
from jax.experimental.pallas import tpu as pltpu
from jax.sharding import Mesh
from jax.sharding import PartitionSpec as P

AXES = ("zl", "y", "zh", "x", "core")
SIZES = (2, 4, 4, 4, 2)
ROW, COL = ("zl", "y"), ("zh", "x", "core")
RING = 4
ROWS = 4096
NB = 256
K = 128
STEP = 1024
PIECES = 8
HIGHEST = lax.Precision.HIGHEST


def tie(a, *events):
    return lax.optimization_barrier((a, *events))[0] if events else a


def shift(a, axis, by):
    n = SIZES[AXES.index(axis)]
    return lax.ppermute(a, axis, [(i, (i + by) % n) for i in range(n)])


def both_ways(a, axis):
    pairs = []
    for i in range(RING):
        pairs.append((i * 2, ((i + 1) % RING) * 2))
        pairs.append((i * 2 + 1, ((i - 1) % RING) * 2 + 1))
    return lax.ppermute(a, (axis, "core"), pairs)


def swap(a):
    return shift(a, "core", 1)


def gather_z(v, other, before=(), between=()):
    n = v.shape[0]
    near = both_ways(tie(jnp.concatenate([v, other], 0), *before), "zh")
    far = both_ways(tie(near[:n], *between), "zh")
    got, got_far = swap(near), swap(far)
    mine = by_block((v, near[:n], near[n:], far))
    theirs = by_block((other, got[:n], got[n:], got_far))
    return mine, theirs, got


def by_block(parts):
    n = parts[0].shape[0] // 8
    return jnp.stack([p.reshape(n, 8, ROWS) for p in parts], 1).reshape(32 * n, ROWS)


def gather_x(mine, theirs, before=(), between=(), after=()):
    near = both_ways(tie(mine, *before), "x")
    near2 = both_ways(tie(theirs, *before), "x")
    far = both_ways(tie(near, *between), "x")
    return (mine, theirs, near, near2, far, swap(near), swap(tie(near2, *after)), swap(tie(far, *after)))


def chunks(n, i):
    return tuple(n * piece + i for piece in range(PIECES))


def column_order(ring):
    z, x, c = (lax.axis_index(a) for a in COL)
    s = 1 - 2 * c

    def half(core, sign):
        if ring:
            return [(z, core), (z - sign, core), (z - sign, 1 - core), (z + 2, core)]
        return [(i, core) for i in range(4)]

    mine, theirs = half(c, s), half(1 - c, -s)
    order = [(x, mine), (x, theirs), (x - s, mine), (x - s, theirs), (x + 2, mine)]
    order += [(x + s, theirs), (x + s, mine), (x + 2, theirs)]
    unit = jnp.stack([((zz % 4) * 4 + xx % 4) * 2 + cc for xx, units in order for zz, cc in units])
    return (unit[:, None] * 8 + jnp.arange(8)[None, :]).reshape(NB)


def exchange(eigvecs):
    return lax.all_to_all(eigvecs.T.reshape(32, K, 128), COL, split_axis=0, concat_axis=0, tiled=True)


def row_share(a):
    n, width = a.shape
    a = lax.all_to_all(a.reshape(8, n // 8, width), ROW, split_axis=0, concat_axis=0, tiled=True)
    return jnp.sum(a, 0)


def hand_on(share):
    n, width = share.shape
    a = jnp.broadcast_to(share, (8, n, width))
    return lax.all_to_all(a, ROW, split_axis=0, concat_axis=0, tiled=True).reshape(8 * n, width)


def row_sum_small(w):
    w = w + shift(w, "zl", 1)
    return w + shift(w, "y", 1) + shift(w, "y", 2) + shift(w, "y", 3)


def split(a):
    hi = a.astype(jnp.bfloat16)
    return hi, (a - hi.astype(jnp.float32)).astype(jnp.bfloat16)


def dot(a, b, dims):
    return lax.dot_general(a, b, (dims, ((), ())), preferred_element_type=jnp.float32)


NT = ((1,), (1,))
NN = ((1,), (0,))


def project(v, cur):
    (vh, vl), (ch, cl) = v, cur
    n = ch.shape[0]
    both = dot(vh, jnp.concatenate([ch, cl], 0), NT)
    return both[:, :n] + both[:, n:] + dot(vl, ch, NT)


def spread_out(applied, v):
    (ah, al), (vh, vl) = applied, v
    both = dot(jnp.concatenate([ah, al], 0), vh, NN)
    return both[:K] + both[K:] + dot(ah, vl, NN)


def stacked(refs):
    return jnp.concatenate([r[...] for r in refs], 0)


def block_of(a, i, n):
    return jnp.concatenate([a[32 * k : 32 * k + 32] for k in chunks(n, i)], 0)


def work_kernel(has_old, has_new, *refs):
    cur_ref, refs = refs[0], refs[1:]
    cur = cur_ref[...] if len(cur_ref.shape) == 2 else jnp.concatenate([cur_ref[i] for i in range(STEP // 128)], 1)
    if has_old:
        applied, old, refs = split(refs[0][...]), split(stacked(refs[1 : 1 + PIECES])), refs[1 + PIECES :]
        cur = cur - spread_out(applied, old)
    if not has_new:
        refs[0][...] = cur.T
        return
    new, refs = stacked(refs[:PIECES]), refs[PIECES:]
    if has_old:
        refs[0][...] = cur
        refs = refs[1:]
    w_ref = refs[0]
    if new.shape[0] == NB:
        part = project(split(new), split(cur))
    else:
        high, low = split(new)
        first, second = ((block_of(high, i, 2), block_of(low, i, 2)) for i in range(2))
        now = split(cur)
        g = project(second, first)
        part = jnp.concatenate([project(first, now), project(second, now), g[:, :K], g[:, K:]], 0)

    @pl.when(pl.program_id(0) == 0)
    def _():
        w_ref[...] = part

    @pl.when(pl.program_id(0) != 0)
    def _():
        w_ref[...] += part


def piece_specs(pieces):
    return [pl.BlockSpec((p.shape[0], STEP), lambda i: (0, i)) for p in pieces]


def rows_of(pieces):
    return sum(p.shape[0] for p in pieces)


def work(cur, applied, old, new):
    args, specs = [cur], [pl.BlockSpec((K, STEP), lambda i: (0, i))]
    if cur.ndim == 3:
        specs = [pl.BlockSpec((STEP // 128, K, 128), lambda i: (i, 0, 0))]
    if old:
        args += [applied, *old]
        specs += [pl.BlockSpec(applied.shape, lambda i: (0, 0))] + piece_specs(old)
    args += new
    specs += piece_specs(new)
    shapes, outs = [], []
    if not new:
        shapes.append(jax.ShapeDtypeStruct((ROWS, K), jnp.float32))
        outs.append(pl.BlockSpec((STEP, K), lambda i: (i, 0)))
    elif old:
        shapes.append(jax.ShapeDtypeStruct((K, ROWS), jnp.float32))
        outs.append(pl.BlockSpec((K, STEP), lambda i: (0, i)))
    if new:
        n = 1024 if rows_of(new) > NB else NB
        shapes.append(jax.ShapeDtypeStruct((n, K), jnp.float32))
        outs.append(pl.BlockSpec((n, K), lambda i: (0, 0)))
    n = rows_of(old) + rows_of(new)
    return pl.pallas_call(
        functools.partial(work_kernel, bool(old), bool(new)),
        grid=(ROWS // STEP,),
        in_specs=specs,
        out_specs=outs,
        out_shape=shapes,
        compiler_params=pltpu.CompilerParams(vmem_limit_bytes=50 << 20),
        cost_estimate=pl.CostEstimate(
            flops=6 * n * K * ROWS, bytes_accessed=4 * ROWS * (n + 2 * K), transcendentals=0
        ),
        name="work",
    )(*args)


def exact(a, b):
    return lax.dot_general(a, b, (NN, ((), ())), precision=HIGHEST, preferred_element_type=jnp.float32)


def solve_kernel(n, t_ref, w_ref, out):
    done = [exact(t_ref[0], w_ref[:NB])]
    if n == 2:
        g = exact(w_ref[2 * NB : 3 * NB], done[0][:K]) + exact(w_ref[3 * NB :], done[0][K:])
        done.append(exact(t_ref[1], w_ref[NB : 2 * NB] - g))
    laid = sorted((k, i, j) for i in range(n) for j, k in enumerate(chunks(n, i)))
    out[...] = jnp.concatenate([done[i][32 * j : 32 * j + 32] for _, i, j in laid], 0).T


def solve(t, w):
    n = t.shape[0]
    return pl.pallas_call(
        functools.partial(solve_kernel, n),
        out_shape=jax.ShapeDtypeStruct((K, NB * n), jnp.float32),
        cost_estimate=pl.CostEstimate(flops=12 * n * NB * NB * K, bytes_accessed=1 << 20, transcendentals=0),
        compiler_params=pltpu.CompilerParams(vmem_limit_bytes=24 << 20),
        name="solve",
    )(t, w)


def on_device(eigvecs, householder, tfactor):
    v = jnp.swapaxes(householder, 1, 2)

    v43, v21 = jnp.concatenate([v[4], v[3]], 0), jnp.concatenate([v[2], v[1]], 0)
    ring43 = gather_z(v43, swap(v43))
    cur = exchange(tie(eigvecs, ring43[2]))
    pieces43 = gather_x(*ring43[:2])
    near43, far43 = pieces43[2], pieces43[4]
    ring21 = gather_z(v21, swap(v21), (ring43[1],), (near43, cur))
    (w,) = work(cur, None, (), pieces43)
    share = row_share(w)
    total = hand_on(share)
    pieces21 = gather_x(*ring21[:2], (far43,), (), (total,))
    near21, far21 = pieces21[3], pieces21[4]
    ring0 = gather_z(v[0], swap(v[0]), (far43,), (total,))
    pieces0 = gather_x(*ring0[:2], (near21,), (far21,))

    def ordered(ring, *blocks):
        pick = (column_order(ring)[:, None] == jnp.arange(NB)[None, :]).astype(jnp.float32)
        part = jnp.stack([tfactor[b] for b in blocks])
        return jnp.einsum("ij,bjk,lk->bil", pick, part, pick, precision=HIGHEST)

    applied = solve(ordered(True, 4, 3), total)
    cur, w = work(cur, applied, pieces43, pieces21)
    applied = solve(ordered(True, 2, 1), hand_on(row_share(w)))
    cur, w = work(cur, applied, pieces21, pieces0)
    applied = solve(ordered(True, 0), row_sum_small(w))
    return work(cur, applied, pieces0, ())[0]


def solution(mesh):
    fine = Mesh(mesh.devices.reshape(SIZES), AXES)
    placed = (P(ROW + COL, None), P(None, ROW, COL), P())
    return jax.shard_map(on_device, mesh=fine, in_specs=placed, out_specs=P(ROW, COL), check_vma=False)
```

```python
import functools

import jax
import jax.numpy as jnp
from jax import lax
from jax.experimental import pallas as pl
from jax.experimental.pallas import tpu as pltpu
from jax.sharding import Mesh
from jax.sharding import PartitionSpec as P

AXES = ("zl", "y", "zh", "x", "core")
SIZES = (2, 4, 4, 4, 2)
ROW, COL = ("zl", "y"), ("zh", "x", "core")
RING = 4
ROWS = 4096
NB = 256
K = 128
STEP = 1024
PIECES = 8
HIGHEST = lax.Precision.HIGHEST


def tie(a, *events):
    return lax.optimization_barrier((a, *events))[0] if events else a


def shift(a, axis, by):
    n = SIZES[AXES.index(axis)]
    return lax.ppermute(a, axis, [(i, (i + by) % n) for i in range(n)])


def both_ways(a, axis):
    pairs = []
    for i in range(RING):
        pairs.append((i * 2, ((i + 1) % RING) * 2))
        pairs.append((i * 2 + 1, ((i - 1) % RING) * 2 + 1))
    return lax.ppermute(a, (axis, "core"), pairs)


def swap(a):
    return shift(a, "core", 1)


def gather_z(v, other, before=(), between=()):
    n = v.shape[0]
    near = both_ways(tie(jnp.concatenate([v, other], 0), *before), "zh")
    far = both_ways(tie(near[:n], *between), "zh")
    got, got_far = swap(near), swap(far)
    mine = by_block((v, near[:n], near[n:], far))
    theirs = by_block((other, got[:n], got[n:], got_far))
    return mine, theirs, got


def by_block(parts):
    n = parts[0].shape[0] // 8
    return jnp.stack([p.reshape(n, 8, ROWS) for p in parts], 1).reshape(32 * n, ROWS)


def gather_x(mine, theirs, before=(), between=(), after=()):
    near = both_ways(tie(mine, *before), "x")
    near2 = both_ways(tie(theirs, *before), "x")
    far = both_ways(tie(near, *between), "x")
    return (mine, theirs, near, near2, far, swap(near), swap(tie(near2, *after)), swap(tie(far, *after)))


def chunks(n, i):
    return tuple(n * piece + i for piece in range(PIECES))


def column_order(ring):
    z, x, c = (lax.axis_index(a) for a in COL)
    s = 1 - 2 * c

    def half(core, sign):
        if ring:
            return [(z, core), (z - sign, core), (z - sign, 1 - core), (z + 2, core)]
        return [(i, core) for i in range(4)]

    mine, theirs = half(c, s), half(1 - c, -s)
    order = [(x, mine), (x, theirs), (x - s, mine), (x - s, theirs), (x + 2, mine)]
    order += [(x + s, theirs), (x + s, mine), (x + 2, theirs)]
    unit = jnp.stack([((zz % 4) * 4 + xx % 4) * 2 + cc for xx, units in order for zz, cc in units])
    return (unit[:, None] * 8 + jnp.arange(8)[None, :]).reshape(NB)


def exchange(eigvecs):
    return lax.all_to_all(eigvecs.T.reshape(32, K, 128), COL, split_axis=0, concat_axis=0, tiled=True)


def row_share(a):
    n, width = a.shape
    a = lax.all_to_all(a.reshape(8, n // 8, width), ROW, split_axis=0, concat_axis=0, tiled=True)
    return jnp.sum(a, 0)


def hand_on(share):
    n, width = share.shape
    a = jnp.broadcast_to(share, (8, n, width))
    return lax.all_to_all(a, ROW, split_axis=0, concat_axis=0, tiled=True).reshape(8 * n, width)


def row_sum_small(w):
    w = w + shift(w, "zl", 1)
    return w + shift(w, "y", 1) + shift(w, "y", 2) + shift(w, "y", 3)


def split(a):
    hi = a.astype(jnp.bfloat16)
    return hi, (a - hi.astype(jnp.float32)).astype(jnp.bfloat16)


def dot(a, b, dims):
    return lax.dot_general(a, b, (dims, ((), ())), preferred_element_type=jnp.float32)


NT = ((1,), (1,))
NN = ((1,), (0,))


def project(v, cur):
    (vh, vl), (ch, cl) = v, cur
    n = ch.shape[0]
    both = dot(vh, jnp.concatenate([ch, cl], 0), NT)
    return both[:, :n] + both[:, n:] + dot(vl, ch, NT)


def spread_out(applied, v):
    (ah, al), (vh, vl) = applied, v
    both = dot(jnp.concatenate([ah, al], 0), vh, NN)
    return both[:K] + both[K:] + dot(ah, vl, NN)


def stacked(refs):
    return jnp.concatenate([r[...] for r in refs], 0)


def block_of(a, i, n):
    return jnp.concatenate([a[32 * k : 32 * k + 32] for k in chunks(n, i)], 0)


def work_kernel(has_old, has_new, *refs):
    cur_ref, refs = refs[0], refs[1:]
    cur = cur_ref[...] if len(cur_ref.shape) == 2 else jnp.concatenate([cur_ref[i] for i in range(STEP // 128)], 1)
    if has_old:
        applied, old, refs = split(refs[0][...]), split(stacked(refs[1 : 1 + PIECES])), refs[1 + PIECES :]
        cur = cur - spread_out(applied, old)
    if not has_new:
        refs[0][...] = cur.T
        return
    new, refs = stacked(refs[:PIECES]), refs[PIECES:]
    if has_old:
        refs[0][...] = cur
        refs = refs[1:]
    w_ref = refs[0]
    if new.shape[0] == NB:
        part = project(split(new), split(cur))
    else:
        high, low = split(new)
        first, second = ((block_of(high, i, 2), block_of(low, i, 2)) for i in range(2))
        now = split(cur)
        g = project(second, first)
        part = jnp.concatenate([project(first, now), project(second, now), g[:, :K], g[:, K:]], 0)

    @pl.when(pl.program_id(0) == 0)
    def _():
        w_ref[...] = part

    @pl.when(pl.program_id(0) != 0)
    def _():
        w_ref[...] += part


def piece_specs(pieces):
    return [pl.BlockSpec((p.shape[0], STEP), lambda i: (0, i)) for p in pieces]


def rows_of(pieces):
    return sum(p.shape[0] for p in pieces)


def work(cur, applied, old, new):
    args, specs = [cur], [pl.BlockSpec((K, STEP), lambda i: (0, i))]
    if cur.ndim == 3:
        specs = [pl.BlockSpec((STEP // 128, K, 128), lambda i: (i, 0, 0))]
    if old:
        args += [applied, *old]
        specs += [pl.BlockSpec(applied.shape, lambda i: (0, 0))] + piece_specs(old)
    args += new
    specs += piece_specs(new)
    shapes, outs = [], []
    if not new:
        shapes.append(jax.ShapeDtypeStruct((ROWS, K), jnp.float32))
        outs.append(pl.BlockSpec((STEP, K), lambda i: (i, 0)))
    elif old:
        shapes.append(jax.ShapeDtypeStruct((K, ROWS), jnp.float32))
        outs.append(pl.BlockSpec((K, STEP), lambda i: (0, i)))
    if new:
        n = 1024 if rows_of(new) > NB else NB
        shapes.append(jax.ShapeDtypeStruct((n, K), jnp.float32))
        outs.append(pl.BlockSpec((n, K), lambda i: (0, 0)))
    n = rows_of(old) + rows_of(new)
    return pl.pallas_call(
        functools.partial(work_kernel, bool(old), bool(new)),
        grid=(ROWS // STEP,),
        in_specs=specs,
        out_specs=outs,
        out_shape=shapes,
        compiler_params=pltpu.CompilerParams(vmem_limit_bytes=50 << 20),
        cost_estimate=pl.CostEstimate(
            flops=6 * n * K * ROWS, bytes_accessed=4 * ROWS * (n + 2 * K), transcendentals=0
        ),
        name="work",
    )(*args)


def exact(a, b):
    return lax.dot_general(a, b, (NN, ((), ())), precision=HIGHEST, preferred_element_type=jnp.float32)


def solve_kernel(n, t_ref, w_ref, out):
    done = [exact(t_ref[0], w_ref[:NB])]
    if n == 2:
        g = exact(w_ref[2 * NB : 3 * NB], done[0][:K]) + exact(w_ref[3 * NB :], done[0][K:])
        done.append(exact(t_ref[1], w_ref[NB : 2 * NB] - g))
    laid = sorted((k, i, j) for i in range(n) for j, k in enumerate(chunks(n, i)))
    out[...] = jnp.concatenate([done[i][32 * j : 32 * j + 32] for _, i, j in laid], 0).T


def solve(t, w):
    n = t.shape[0]
    return pl.pallas_call(
        functools.partial(solve_kernel, n),
        out_shape=jax.ShapeDtypeStruct((K, NB * n), jnp.float32),
        cost_estimate=pl.CostEstimate(flops=12 * n * NB * NB * K, bytes_accessed=1 << 20, transcendentals=0),
        compiler_params=pltpu.CompilerParams(vmem_limit_bytes=24 << 20),
        name="solve",
    )(t, w)


def on_device(eigvecs, householder, tfactor):
    v = jnp.swapaxes(householder, 1, 2)

    v43, v21 = jnp.concatenate([v[4], v[3]], 0), jnp.concatenate([v[2], v[1]], 0)
    ring43 = gather_z(v43, swap(v43))
    cur = exchange(tie(eigvecs, ring43[2]))
    pieces43 = gather_x(*ring43[:2])
    near43, far43 = pieces43[2], pieces43[4]
    ring21 = gather_z(v21, swap(v21), (ring43[1],), (near43, cur))
    (w,) = work(cur, None, (), pieces43)
    share = row_share(w)
    total = hand_on(share)
    pieces21 = gather_x(*ring21[:2], (far43,), (), (total,))
    far21 = pieces21[4]
    ring0 = gather_z(v[0], swap(v[0]), (far43,), (total,))

    def ordered(ring, *blocks):
        pick = (column_order(ring)[:, None] == jnp.arange(NB)[None, :]).astype(jnp.float32)
        part = jnp.stack([tfactor[b] for b in blocks])
        return jnp.einsum("ij,bjk,lk->bil", pick, part, pick, precision=HIGHEST)

    applied = solve(ordered(True, 4, 3), total)
    cur, w = work(cur, applied, pieces43, pieces21)
    pieces0 = gather_x(*ring0[:2], (w,), (far21,))
    applied = solve(ordered(True, 2, 1), hand_on(row_share(w)))
    cur, w = work(cur, applied, pieces21, pieces0)
    applied = solve(ordered(True, 0), row_sum_small(w))
    return work(cur, applied, pieces0, ())[0]


def solution(mesh):
    fine = Mesh(mesh.devices.reshape(SIZES), AXES)
    placed = (P(ROW + COL, None), P(None, ROW, COL), P())
    return jax.shard_map(on_device, mesh=fine, in_specs=placed, out_specs=P(ROW, COL), check_vma=False)
```
